32 devices in a mesh: seq: 8 (over z, y), chan: 4 (over x, core).
Axes of the slice: x: 2, y: 2, z: 4, core: 2. Of those that a mesh axis runs over, the one named last changes fastest.
Arguments:
- q_proj: bfloat16 [1024, 8192], P('seq', 'chan'), may hold values from -6 to 6
- k_proj: bfloat16 [1024, 8192], P('seq', 'chan'), may hold values from -6 to 6
- v_proj: bfloat16 [1024, 8192], P('seq', 'chan'), may hold values from -6 to 6
- residues: float32 [8192, 16], P('chan'), may hold values from -1.5 to 1.5
- rates: float32 [8192, 16], P('chan'), may hold values from 0.5 to 32
- skip_gain: float32 [8192], P('chan'), may hold values from -4 to 4
- w_out: bfloat16 [8192, 8192], P('chan', 'seq'), may hold values from -0.0625 to 0.0625
Outputs:
- mixed: bfloat16 [1024, 8192], P('seq', 'chan')
The draws below stay inside these ranges and needn't reach their ends.
All inputs are finite; a program needn't handle non-finite values.
Results may differ from the reference program's by a relative error of at most 0.0085.
Values may be sent and summed in bfloat16 or wider, within the bound.
No kernel may reach another device: no remote copies, remote signals or barrier semaphores. Data moves between devices by JAX's collectives and lax.ppermute only.
A program may use at most 128 MiB of HBM per device.

```python
import math
import jax
import jax.numpy as jnp

D = 8192
CH = 8192
MODES = 16
TOKENS = 1024


def level_of(rng, extent, cuts, low, high):
    def one(axis_at, shards_of):
        draws = jax.random.uniform(jax.random.fold_in(jax.random.fold_in(rng, 6), axis_at), (shards_of,), jnp.float32, low / len(cuts), high / len(cuts))
        return jnp.repeat(jnp.exp(draws), extent[axis_at] // shards_of).reshape((-1,) + (1,) * (len(extent) - axis_at - 1))

    gain = one(*cuts[0])
    for cut in cuts[1:]:
        gain = gain * one(*cut)
    return gain


def gaussian(key, dims, spread, reach, split=(), kind=jnp.bfloat16):
    result = jax.random.normal(key, dims, jnp.float32) * spread
    if len(split) > 0:
        result = level_of(key, dims, split, -0.22, 0.18) * result
    return jnp.clip(result, min=-reach, max=reach).astype(kind)


def setup_inputs(seed: int = 0) -> dict:
    key_list = jax.random.split(jax.random.key(seed), 8)
    return {
        "q_proj": gaussian(key_list[0], (TOKENS, CH), 1.0, 6.0, ((0, 8), (1, 4))),
        "k_proj": gaussian(key_list[1], (TOKENS, CH), 1.0, 6.0, ((0, 8), (1, 4))),
        "v_proj": gaussian(key_list[2], (TOKENS, CH), 1.0, 6.0, ((0, 8), (1, 4))),
        "residues": gaussian(key_list[3], (CH, MODES), MODES ** -0.5, 1.5, ((0, 4),), jnp.float32),
        "rates": jnp.clip(jnp.exp(math.log(32.0) - 4.158883 * jax.random.uniform(key_list[4], (CH, MODES), jnp.float32) ** level_of(key_list[4], (CH, MODES), ((0, 4),), -0.2, 0.2)), 0.5, 32.0),
        "skip_gain": gaussian(key_list[5], (CH,), 1.0, 4.0, ((0, 4),), jnp.float32),
        "w_out": gaussian(key_list[6], (CH, D), CH ** -0.5, 0.0625, ((0, 4), (1, 8))),
    }


def conv_block(source, residues, rates):
    places = jnp.arange(TOKENS, dtype=jnp.int32).astype(jnp.float32)
    taps = jnp.zeros(source.shape, jnp.float32)
    for mode in range(MODES):
        weight = residues[:, mode] * jnp.sqrt(2.0 * rates[:, mode] / TOKENS)
        decay = jnp.exp(-(rates[:, mode][None, :] * places[:, None]) / TOKENS)
        taps = taps + weight[None, :] * decay
    length = 2 * TOKENS
    spectrum = jnp.fft.rfft(source, n=length, axis=0) * jnp.fft.rfft(taps, n=length, axis=0)
    return jnp.fft.irfft(spectrum, n=length, axis=0)[:TOKENS].astype(jnp.float32)

def reference(q_proj, k_proj, v_proj, residues, rates, skip_gain, w_out):
    block = min(CH, 1024)
    pieces = []
    for first in range(0, CH, block):
        source = k_proj[:, first:first + block].astype(jnp.float32) * v_proj[:, first:first + block].astype(jnp.float32)
        conv = conv_block(source, residues[first:first + block], rates[first:first + block])
        gated = q_proj[:, first:first + block].astype(jnp.float32) * (conv + skip_gain[first:first + block][None, :] * source)
        pieces.append(gated.astype(jnp.bfloat16))
    hidden = jnp.concatenate(pieces, axis=1)
    return jnp.dot(hidden, w_out, preferred_element_type=jnp.float32).astype(jnp.bfloat16)
```

```python
import functools

import jax
import jax.numpy as jnp
from jax import lax
from jax.experimental import pallas as pl
from jax.experimental.pallas import tpu as pltpu
from jax.sharding import PartitionSpec as P

BF16 = jnp.bfloat16
F32 = jnp.float32
SUB = 8
LANES = 128
BOTH = ("seq", "chan")


def spread_rows(row):
    return jnp.broadcast_to(row, (SUB, row.shape[-1]))


def source_rows(k_ref, v_ref, x_ref, lanes):
    x_ref[...] = k_ref[:, lanes].astype(F32) * v_ref[:, lanes].astype(F32)
    length = x_ref.shape[0] // SUB
    return [x_ref[pl.ds(i, SUB, stride=length), :] for i in range(length)]


def state_kernel(total, k_ref, v_ref, rate_ref, state_ref, x_ref):
    modes, width = rate_ref.shape
    length = x_ref.shape[0] // SUB
    block = lax.broadcasted_iota(jnp.int32, (SUB, LANES), 0).astype(F32)

    @pl.loop(0, width // LANES)
    def _(chunk):
        lanes = pl.ds(pl.multiple_of(chunk * LANES, LANES), LANES)
        x = source_rows(k_ref, v_ref, x_ref, lanes)
        rate = rate_ref[:, lanes] * (-1.0 / total)
        decay = jnp.exp(rate)
        rows = []
        for m in range(modes):
            d = spread_rows(decay[m : m + 1])
            state = x[0]
            for i in range(1, length):
                state = state * d + x[i]
            weight = jnp.exp(spread_rows(rate[m : m + 1]) * ((SUB - 1.0 - block) * length))
            rows.append(jnp.sum(state * weight, axis=0, keepdims=True))
        state_ref[:, lanes] = jnp.concatenate(rows, axis=0)


def local_kernel(total, q_ref, k_ref, v_ref, res_ref, rate_ref, skip_ref, base_ref, x_ref, y_ref):
    modes, width = rate_ref.shape
    length = x_ref.shape[0] // SUB
    block = lax.broadcasted_iota(jnp.int32, (SUB, LANES), 0)

    @pl.loop(0, width // LANES)
    def _(chunk):
        lanes = pl.ds(pl.multiple_of(chunk * LANES, LANES), LANES)
        x = source_rows(k_ref, v_ref, x_ref, lanes)
        rate = rate_ref[:, lanes] * (-1.0 / total)
        gain = res_ref[:, lanes] * jnp.sqrt(rate_ref[:, lanes] * (2.0 / total))
        decay = jnp.exp(rate)
        y = [spread_rows(skip_ref[:, lanes]) * x[i] for i in range(length)]
        power = gain
        for j in range(length):
            tap = spread_rows(jnp.sum(power, axis=0, keepdims=True))
            for i in range(j, length):
                y[i] = y[i] + tap * x[i - j]
            power = power * decay
        for m in range(modes):
            d = spread_rows(decay[m : m + 1])
            state = x[0]
            for i in range(1, length):
                state = state * d + x[i]
            step = spread_rows(rate[m : m + 1]) * length
            state = jnp.where(block >= 1, pltpu.roll(state, 1, 0), 0.0)
            for shift in (1, 2, 4):
                moved = jnp.where(block >= shift, pltpu.roll(state, shift, 0), 0.0)
                state = state + jnp.exp(step * shift) * moved
            state = state * spread_rows(gain[m : m + 1])
            for i in range(length):
                state = state * d
                y[i] = y[i] + state
        for i in range(length):
            y_ref[pl.ds(i, SUB, stride=length), :] = y[i]
        base_ref[:, lanes] = y_ref[...] * q_ref[:, lanes].astype(F32)


def carry_kernel(total, q_ref, base_ref, state_ref, res_ref, rate_ref, out_ref, y_ref):
    modes, width = rate_ref.shape
    length = y_ref.shape[0] // SUB
    block = lax.broadcasted_iota(jnp.int32, (SUB, LANES), 0).astype(F32)

    @pl.loop(0, width // LANES)
    def _(chunk):
        lanes = pl.ds(pl.multiple_of(chunk * LANES, LANES), LANES)
        rate = rate_ref[:, lanes] * (-1.0 / total)
        start = state_ref[:, lanes] * res_ref[:, lanes] * jnp.sqrt(rate_ref[:, lanes] * (2.0 / total))
        decay = jnp.exp(rate)
        y = [jnp.zeros((SUB, LANES), F32) for i in range(length)]
        for m in range(modes):
            d = spread_rows(decay[m : m + 1])
            state = spread_rows(start[m : m + 1]) * jnp.exp(spread_rows(rate[m : m + 1]) * (block * length))
            for i in range(length):
                state = state * d
                y[i] = y[i] + state
        for i in range(length):
            y_ref[pl.ds(i, SUB, stride=length), :] = y[i]
        out_ref[:, lanes] = (base_ref[:, lanes] + y_ref[...] * q_ref[:, lanes].astype(F32)).astype(BF16)


def run(kernel, out, scratch, ops, *args):
    rows, width = args[0].shape
    return pl.pallas_call(
        kernel,
        out_shape=out,
        in_specs=[pl.BlockSpec(memory_space=pltpu.VMEM)] * len(args),
        out_specs=pl.BlockSpec(memory_space=pltpu.VMEM),
        scratch_shapes=[pltpu.VMEM((rows, LANES), F32)] * scratch,
        compiler_params=pltpu.CompilerParams(vmem_limit_bytes=32 * 1024 * 1024),
        cost_estimate=pl.CostEstimate(
            flops=ops * rows * width, bytes_accessed=6 * rows * width, transcendentals=0
        ),
    )(*args)


def matmul(x, w):
    return jnp.dot(x, w, preferred_element_type=F32)


def general(hidden_of, state, w_out, fade, rows, index, parts):
    states = lax.all_gather(state.astype(BF16), "seq", axis=0)
    entering = jnp.zeros(state.shape, F32)
    for b in range(parts):
        entering = jnp.where(b < index, entering * fade(rows) + states[b].astype(F32), entering)
    hidden = hidden_of(entering)
    spread = matmul(lax.all_gather(hidden, "seq", axis=0, tiled=True), w_out)
    partial_value = lax.all_to_all(spread, "seq", split_axis=0, concat_axis=1, tiled=True)
    summed = lax.psum_scatter(partial_value, "chan", scatter_dimension=1, tiled=True)
    return summed.astype(BF16)


def lined(hidden_of, state, w_out, fade, rows, index):
    depth = 4
    z, y = index // 2, index % 2

    def along(x, moves):
        return lax.ppermute(x, "seq", [(a * 2 + b, c * 2 + b) for a, c in moves for b in range(2)])

    def across(x, planes):
        return lax.ppermute(x, "seq", [(a * 2 + b, a * 2 + 1 - b) for a in planes for b in range(2)])

    def shift(by):
        return [(a, a + by) for a in range(depth) if 0 <= a + by < depth]

    every = range(depth)
    own = state.astype(BF16)
    other = across(own, every)
    first = jnp.where(y == 0, own, other).astype(F32)
    second = jnp.where(y == 0, other, own).astype(F32)
    plane = (first * fade(rows) + second).astype(BF16)
    entering = jnp.zeros(state.shape, F32)
    for by in range(1, depth):
        entering = entering + along(plane, shift(by)).astype(F32) * fade(2 * rows * (by - 1))
    entering = jnp.where(y == 0, entering, entering * fade(rows) + first)
    hidden = hidden_of(entering)

    up1 = along(hidden, shift(1))
    down1 = along(hidden, shift(-1))
    far2 = along(up1, [(1, 2), (2, 3)]) + along(down1, [(1, 0), (2, 1)])
    far3 = along(far2, [(1, 0), (2, 3)])
    swap = {0: 2, 1: 3, 2: 0, 3: 1}
    slots = [
        (hidden, [(a, a) for a in every]),
        (up1, shift(-1)),
        (down1, shift(1)),
        (far2, list(swap.items())),
        (far3, [(0, 3), (3, 0)]),
    ]
    gathered = []
    for block, moves in slots:
        gathered.append((block, moves, 0))
        gathered.append((across(block, [a for a, c in moves]), moves, 1))

    root = (lax.axis_index("chan") % 2) == (z % 2)
    sums = [0.0, 0.0]
    for block, moves, dy in gathered:
        part = matmul(block, w_out)
        pairs = [
            ((a * 2 + b) * 4 + x * 2 + 1 - a % 2, (a * 2 + b) * 4 + x * 2 + a % 2)
            for a, c in moves
            for b in range(2)
            for x in range(2)
        ]
        pair_sum = (part + lax.ppermute(part.astype(BF16), BOTH, pairs).astype(F32)).astype(BF16)
        for side in range(2):
            pairs = [
                (
                    (a * 2 + b) * 4 + ((a // 2) ^ side) * 2 + a % 2,
                    (c * 2 + (b ^ dy)) * 4 + a,
                )
                for a, c in moves
                for b in range(2)
            ]
            sums[dy] = sums[dy] + lax.ppermute(pair_sum, BOTH, pairs).astype(F32)
    low = jnp.where(y == 0, sums[0], sums[1])
    high = jnp.where(y == 0, sums[1], sums[0])
    return jnp.concatenate([low, high], axis=1).astype(BF16)


def local(q_proj, k_proj, v_proj, residues, rates, skip_gain, w_out):
    rows, width = q_proj.shape
    parts = lax.axis_size("seq")
    index = lax.axis_index("seq")
    total = rows * parts
    modes = rates.shape[1]
    res_t, rate_t = residues.T, rates.T
    state = run(
        functools.partial(state_kernel, total),
        jax.ShapeDtypeStruct((modes, width), F32),
        1,
        48,
        k_proj,
        v_proj,
        rate_t,
    )
    base = run(
        functools.partial(local_kernel, total),
        jax.ShapeDtypeStruct((rows, width), F32),
        2,
        100,
        q_proj,
        k_proj,
        v_proj,
        res_t,
        rate_t,
        skip_gain[None, :],
    )

    def hidden_of(entering):
        return run(
            functools.partial(carry_kernel, total),
            jax.ShapeDtypeStruct((rows, width), BF16),
            1,
            32,
            q_proj,
            base,
            entering,
            res_t,
            rate_t,
        )

    def fade(steps):
        return jnp.exp(rate_t * (-float(steps) / total))

    if parts == 8 and lax.axis_size("chan") == 4:
        return lined(hidden_of, state, w_out, fade, rows, index)
    return general(hidden_of, state, w_out, fade, rows, index, parts)


def solution(mesh):
    return jax.shard_map(
        local,
        mesh=mesh,
        in_specs=(
            P("seq", "chan"),
            P("seq", "chan"),
            P("seq", "chan"),
            P("chan", None),
            P("chan", None),
            P("chan"),
            P("chan", "seq"),
        ),
        out_specs=P("seq", "chan"),
        check_vma=False,
    )
```

```python
import functools

import jax
import jax.numpy as jnp
from jax import lax
from jax.experimental import pallas as pl
from jax.experimental.pallas import tpu as pltpu
from jax.sharding import PartitionSpec as P

BF16 = jnp.bfloat16
F32 = jnp.float32
SUB = 8
LANES = 128
BOTH = ("seq", "chan")


def spread_rows(row):
    return jnp.broadcast_to(row, (SUB, row.shape[-1]))


def source_rows(k_ref, v_ref, x_ref, lanes):
    x_ref[...] = k_ref[:, lanes].astype(F32) * v_ref[:, lanes].astype(F32)
    length = x_ref.shape[0] // SUB
    return [x_ref[pl.ds(i, SUB, stride=length), :] for i in range(length)]


def state_kernel(total, k_ref, v_ref, rate_ref, state_ref, x_ref):
    modes, width = rate_ref.shape
    length = x_ref.shape[0] // SUB
    block = lax.broadcasted_iota(jnp.int32, (SUB, LANES), 0).astype(F32)

    @pl.loop(0, width // LANES)
    def _(chunk):
        lanes = pl.ds(pl.multiple_of(chunk * LANES, LANES), LANES)
        x = source_rows(k_ref, v_ref, x_ref, lanes)
        rate = rate_ref[:, lanes] * (-1.0 / total)
        decay = jnp.exp(rate)
        rows = []
        for m in range(modes):
            d = spread_rows(decay[m : m + 1])
            state = x[0]
            for i in range(1, length):
                state = state * d + x[i]
            weight = jnp.exp(spread_rows(rate[m : m + 1]) * ((SUB - 1.0 - block) * length))
            rows.append(jnp.sum(state * weight, axis=0, keepdims=True))
        state_ref[:, lanes] = jnp.concatenate(rows, axis=0)


def local_kernel(total, q_ref, k_ref, v_ref, res_ref, rate_ref, skip_ref, base_ref, x_ref, y_ref):
    modes, width = rate_ref.shape
    length = x_ref.shape[0] // SUB
    block = lax.broadcasted_iota(jnp.int32, (SUB, LANES), 0)

    @pl.loop(0, width // LANES)
    def _(chunk):
        lanes = pl.ds(pl.multiple_of(chunk * LANES, LANES), LANES)
        x = source_rows(k_ref, v_ref, x_ref, lanes)
        rate = rate_ref[:, lanes] * (-1.0 / total)
        gain = res_ref[:, lanes] * jnp.sqrt(rate_ref[:, lanes] * (2.0 / total))
        decay = jnp.exp(rate)
        y = [spread_rows(skip_ref[:, lanes]) * x[i] for i in range(length)]
        power = gain
        for j in range(length):
            tap = spread_rows(jnp.sum(power, axis=0, keepdims=True))
            for i in range(j, length):
                y[i] = y[i] + tap * x[i - j]
            power = power * decay
        for m in range(modes):
            d = spread_rows(decay[m : m + 1])
            state = x[0]
            for i in range(1, length):
                state = state * d + x[i]
            step = spread_rows(rate[m : m + 1]) * length
            state = jnp.where(block >= 1, pltpu.roll(state, 1, 0), 0.0)
            for shift in (1, 2, 4):
                moved = jnp.where(block >= shift, pltpu.roll(state, shift, 0), 0.0)
                state = state + jnp.exp(step * shift) * moved
            state = state * spread_rows(gain[m : m + 1])
            for i in range(length):
                state = state * d
                y[i] = y[i] + state
        for i in range(length):
            y_ref[pl.ds(i, SUB, stride=length), :] = y[i]
        base_ref[:, lanes] = y_ref[...] * q_ref[:, lanes].astype(F32)


def carry_kernel(total, q_ref, base_ref, state_ref, res_ref, rate_ref, out_ref, y_ref):
    modes, width = rate_ref.shape
    length = y_ref.shape[0] // SUB
    block = lax.broadcasted_iota(jnp.int32, (SUB, LANES), 0).astype(F32)

    @pl.loop(0, width // LANES)
    def _(chunk):
        lanes = pl.ds(pl.multiple_of(chunk * LANES, LANES), LANES)
        rate = rate_ref[:, lanes] * (-1.0 / total)
        start = state_ref[:, lanes] * res_ref[:, lanes] * jnp.sqrt(rate_ref[:, lanes] * (2.0 / total))
        decay = jnp.exp(rate)
        y = [jnp.zeros((SUB, LANES), F32) for i in range(length)]
        for m in range(modes):
            d = spread_rows(decay[m : m + 1])
            state = spread_rows(start[m : m + 1]) * jnp.exp(spread_rows(rate[m : m + 1]) * (block * length))
            for i in range(length):
                state = state * d
                y[i] = y[i] + state
        for i in range(length):
            y_ref[pl.ds(i, SUB, stride=length), :] = y[i]
        out_ref[:, lanes] = (base_ref[:, lanes] + y_ref[...] * q_ref[:, lanes].astype(F32)).astype(BF16)


def run(kernel, out, scratch, ops, *args):
    rows, width = args[0].shape
    part = min(width, 4 * LANES)
    return pl.pallas_call(
        kernel,
        grid=(width // part,),
        out_shape=out,
        in_specs=[pl.BlockSpec((arg.shape[0], part), lambda i: (0, i)) for arg in args],
        out_specs=pl.BlockSpec((out.shape[0], part), lambda i: (0, i)),
        scratch_shapes=[pltpu.VMEM((rows, LANES), F32)] * scratch,
        compiler_params=pltpu.CompilerParams(vmem_limit_bytes=16 * 1024 * 1024),
        cost_estimate=pl.CostEstimate(
            flops=ops * rows * width, bytes_accessed=6 * rows * width, transcendentals=0
        ),
    )(*args)


def matmul(x, w):
    return jnp.dot(x, w, preferred_element_type=F32)


def general(hidden_of, state, w_out, fade, rows, index, parts):
    states = lax.all_gather(state.astype(BF16), "seq", axis=0)
    entering = jnp.zeros(state.shape, F32)
    for b in range(parts):
        entering = jnp.where(b < index, entering * fade(rows) + states[b].astype(F32), entering)
    hidden = hidden_of(entering)
    spread = matmul(lax.all_gather(hidden, "seq", axis=0, tiled=True), w_out)
    partial_value = lax.all_to_all(spread, "seq", split_axis=0, concat_axis=1, tiled=True)
    summed = lax.psum_scatter(partial_value, "chan", scatter_dimension=1, tiled=True)
    return summed.astype(BF16)


def lined(hidden_of, state, w_out, fade, rows, index):
    depth = 4
    z, y = index // 2, index % 2

    def along(x, moves):
        return lax.ppermute(x, "seq", [(a * 2 + b, c * 2 + b) for a, c in moves for b in range(2)])

    def across(x, planes):
        return lax.ppermute(x, "seq", [(a * 2 + b, a * 2 + 1 - b) for a in planes for b in range(2)])

    def shift(by):
        return [(a, a + by) for a in range(depth) if 0 <= a + by < depth]

    every = range(depth)
    own = state.astype(BF16)
    other = across(own, every)
    first = jnp.where(y == 0, own, other).astype(F32)
    second = jnp.where(y == 0, other, own).astype(F32)
    plane = (first * fade(rows) + second).astype(BF16)
    entering = jnp.zeros(state.shape, F32)
    for by in range(1, depth):
        entering = entering + along(plane, shift(by)).astype(F32) * fade(2 * rows * (by - 1))
    entering = jnp.where(y == 0, entering, entering * fade(rows) + first)
    hidden = hidden_of(entering)

    chan = lax.axis_index("chan")
    side, core = chan // 2, chan % 2
    up1 = along(hidden, shift(1))
    down1 = along(hidden, shift(-1))
    near_y = across(hidden, every)
    one = jnp.where(z % 2 == 1, up1, down1)
    up2 = along(up1, [(1, 2), (2, 3)])
    down2 = along(down1, [(1, 0), (2, 1)])
    one_y = across(one, every)
    two = jnp.where(z >= 2, up2, down2)
    far3 = along(two, [(1, 0), (2, 3)])
    two_y = across(two, every)
    three = jnp.where(z % 3 == 0, far3, jnp.where(z == 1, down1, up1))
    three_y = across(three, every)

    flip = [(c, c ^ 1) for c in range(4)]
    turn = [(c, c ^ 2) for c in range(4)]

    def reduced(group, even, odd):
        even = [matmul(block, w_out) for block in even]
        odd = [matmul(block, w_out) for block in odd]
        keep = jnp.stack([jnp.where(core == 0, a, b) for a, b in zip(even, odd)])
        send = jnp.stack([jnp.where(core == 0, b, a).astype(BF16) for a, b in zip(even, odd)])
        keep = keep + lax.ppermute(send, "chan", flip).astype(F32)
        send = jnp.where(side == 0, keep[1], keep[0]).astype(BF16)
        keep = jnp.where(side == 0, keep[0], keep[1])
        tile = (keep + lax.ppermute(send, "chan", turn).astype(F32)).astype(BF16)
        arrived = []
        for x in range(2):
            pairs = [
                ((a * 2 + b) * 4 + x * 2 + k, ((a ^ (group + k)) * 2 + (b ^ x)) * 4 + a)
                for a in every
                for b in range(2)
                for k in range(2)
            ]
            arrived.append(lax.ppermute(tile, BOTH, pairs))
        return arrived

    close = reduced(0, [hidden, near_y], [one, one_y])
    remote = reduced(2, [two, two_y], [three, three_y])
    close_here = (z ^ chan) < 2
    same = jnp.where(close_here, close[0], remote[0])
    cross = jnp.where(close_here, close[1], remote[1])
    low = jnp.where(y == 0, same, cross)
    high = jnp.where(y == 0, cross, same)
    return jnp.concatenate([low, high], axis=1)


def local(q_proj, k_proj, v_proj, residues, rates, skip_gain, w_out):
    rows, width = q_proj.shape
    parts = lax.axis_size("seq")
    index = lax.axis_index("seq")
    total = rows * parts
    modes = rates.shape[1]
    res_t, rate_t = residues.T, rates.T
    state = run(
        functools.partial(state_kernel, total),
        jax.ShapeDtypeStruct((modes, width), F32),
        1,
        48,
        k_proj,
        v_proj,
        rate_t,
    )
    base = run(
        functools.partial(local_kernel, total),
        jax.ShapeDtypeStruct((rows, width), F32),
        2,
        100,
        q_proj,
        k_proj,
        v_proj,
        res_t,
        rate_t,
        skip_gain[None, :],
    )

    def hidden_of(entering):
        return run(
            functools.partial(carry_kernel, total),
            jax.ShapeDtypeStruct((rows, width), BF16),
            1,
            32,
            q_proj,
            base,
            entering,
            res_t,
            rate_t,
        )

    def fade(steps):
        return jnp.exp(rate_t * (-float(steps) / total))

    if parts == 8 and lax.axis_size("chan") == 4:
        return lined(hidden_of, state, w_out, fade, rows, index)
    return general(hidden_of, state, w_out, fade, rows, index, parts)


def solution(mesh):
    return jax.shard_map(
        local,
        mesh=mesh,
        in_specs=(
            P("seq", "chan"),
            P("seq", "chan"),
            P("seq", "chan"),
            P("chan", None),
            P("chan", None),
            P("chan"),
            P("chan", "seq"),
        ),
        out_specs=P("seq", "chan"),
        check_vma=False,
    )
```

```python
import functools

import jax
import jax.numpy as jnp
from jax import lax
from jax.experimental import pallas as pl
from jax.experimental.pallas import tpu as pltpu
from jax.sharding import PartitionSpec as P

BF16 = jnp.bfloat16
F32 = jnp.float32
SUB = 8
LANES = 128
BOTH = ("seq", "chan")


def spread_rows(row):
    return jnp.broadcast_to(row, (SUB, row.shape[-1]))


def source_rows(k_ref, v_ref, x_ref, lanes):
    x_ref[...] = k_ref[:, lanes].astype(F32) * v_ref[:, lanes].astype(F32)
    length = x_ref.shape[0] // SUB
    return [x_ref[pl.ds(i, SUB, stride=length), :] for i in range(length)]


def state_kernel(total, k_ref, v_ref, rate_ref, state_ref, x_ref):
    modes, width = rate_ref.shape
    length = x_ref.shape[0] // SUB
    block = lax.broadcasted_iota(jnp.int32, (SUB, LANES), 0).astype(F32)

    @pl.loop(0, width // LANES)
    def _(chunk):
        lanes = pl.ds(pl.multiple_of(chunk * LANES, LANES), LANES)
        x = source_rows(k_ref, v_ref, x_ref, lanes)
        rate = rate_ref[:, lanes] * (-1.0 / total)
        decay = jnp.exp(rate)
        rows = []
        for m in range(modes):
            d = spread_rows(decay[m : m + 1])
            state = x[0]
            for i in range(1, length):
                state = state * d + x[i]
            weight = jnp.exp(spread_rows(rate[m : m + 1]) * ((SUB - 1.0 - block) * length))
            rows.append(jnp.sum(state * weight, axis=0, keepdims=True))
        state_ref[:, lanes] = jnp.concatenate(rows, axis=0).astype(BF16)


def local_kernel(total, q_ref, k_ref, v_ref, res_ref, rate_ref, skip_ref, *rest):
    base_ref, x_ref, y_ref = rest[-3:]
    modes, width = rate_ref.shape
    length = x_ref.shape[0] // SUB
    block = lax.broadcasted_iota(jnp.int32, (SUB, LANES), 0)

    @pl.loop(0, width // LANES)
    def _(chunk):
        lanes = pl.ds(pl.multiple_of(chunk * LANES, LANES), LANES)
        x = source_rows(k_ref, v_ref, x_ref, lanes)
        rate = rate_ref[:, lanes] * (-1.0 / total)
        gain = res_ref[:, lanes] * jnp.sqrt(rate_ref[:, lanes] * (2.0 / total))
        decay = jnp.exp(rate)
        y = [spread_rows(skip_ref[:, lanes]) * x[i] for i in range(length)]
        power = gain
        for j in range(length):
            tap = spread_rows(jnp.sum(power, axis=0, keepdims=True))
            for i in range(j, length):
                y[i] = y[i] + tap * x[i - j]
            power = power * decay
        for m in range(modes):
            d = spread_rows(decay[m : m + 1])
            state = x[0]
            for i in range(1, length):
                state = state * d + x[i]
            step = spread_rows(rate[m : m + 1]) * length
            state = jnp.where(block >= 1, pltpu.roll(state, 1, 0), 0.0)
            for shift in (1, 2, 4):
                moved = jnp.where(block >= shift, pltpu.roll(state, shift, 0), 0.0)
                state = state + jnp.exp(step * shift) * moved
            state = state * spread_rows(gain[m : m + 1])
            for i in range(length):
                state = state * d
                y[i] = y[i] + state
        for i in range(length):
            y_ref[pl.ds(i, SUB, stride=length), :] = y[i]
        base_ref[:, lanes] = y_ref[...] * q_ref[:, lanes].astype(F32)


def carry_kernel(total, odd_ref, q_ref, base_ref, below_ref, further_ref, first_ref, res_ref, rate_ref, out_ref, y_ref):
    modes, width = rate_ref.shape
    length = y_ref.shape[0] // SUB
    block = lax.broadcasted_iota(jnp.int32, (SUB, LANES), 0).astype(F32)

    @pl.loop(0, width // LANES)
    def _(chunk):
        lanes = pl.ds(pl.multiple_of(chunk * LANES, LANES), LANES)
        rate = rate_ref[:, lanes] * (-1.0 / total)
        rows = SUB * length
        start = below_ref[:, lanes].astype(F32) + further_ref[:, lanes].astype(F32) * jnp.exp(rate * (2 * rows))
        later = start * jnp.exp(rate * rows) + first_ref[:, lanes].astype(F32)
        start = jnp.where(odd_ref[0] == 1, later, start)
        start = start * res_ref[:, lanes] * jnp.sqrt(rate_ref[:, lanes] * (2.0 / total))
        decay = jnp.exp(rate)
        y = [jnp.zeros((SUB, LANES), F32) for i in range(length)]
        for m in range(modes):
            d = spread_rows(decay[m : m + 1])
            state = spread_rows(start[m : m + 1]) * jnp.exp(spread_rows(rate[m : m + 1]) * (block * length))
            for i in range(length):
                state = state * d
                y[i] = y[i] + state
        for i in range(length):
            y_ref[pl.ds(i, SUB, stride=length), :] = y[i]
        out_ref[:, lanes] = (base_ref[:, lanes] + y_ref[...] * q_ref[:, lanes].astype(F32)).astype(BF16)


def run(kernel, out, scratch, ops, mib, args, window=None, filled=None, scalars=()):
    rows, width = args[0].shape
    part = min(width // 4, 4 * LANES)
    steps = width // part
    first = 0
    if window is not None:
        first, steps = window[0] * steps // 4, (window[1] - window[0]) * steps // 4
    specs = [pl.BlockSpec(memory_space=pltpu.SMEM)] * len(scalars)
    specs += [pl.BlockSpec((arg.shape[0], part), lambda i: (0, i + first)) for arg in args]
    if filled is not None:
        specs.append(pl.BlockSpec(memory_space=pl.ANY))
    return pl.pallas_call(
        kernel,
        grid=(steps,),
        out_shape=out,
        in_specs=specs,
        out_specs=pl.BlockSpec((out.shape[0], part), lambda i: (0, i + first)),
        scratch_shapes=[pltpu.VMEM((rows, LANES), F32)] * scratch,
        input_output_aliases={} if filled is None else {len(specs) - 1: 0},
        compiler_params=pltpu.CompilerParams(vmem_limit_bytes=mib * 1024 * 1024),
        cost_estimate=pl.CostEstimate(
            flops=ops * rows * part * steps, bytes_accessed=6 * rows * part * steps, transcendentals=0
        ),
    )(*scalars, *args, *(() if filled is None else (filled,)))


def matmul(x, w):
    return jnp.dot(x, w, preferred_element_type=F32)


def moved(x, axes, pairs, name):
    with jax.named_scope(name):
        return lax.ppermute(x, axes, pairs)


def fence(*xs):
    return lax.optimization_barrier(xs)


def general(base_of, hidden_of, state, w_out, fade, rows, index, parts):
    states = lax.all_gather(state, "seq", axis=0)
    entering = jnp.zeros(state.shape, F32)
    for b in range(parts):
        entering = jnp.where(b < index, entering * fade(rows) + states[b].astype(F32), entering)
    nothing = jnp.zeros_like(state)
    hidden = hidden_of(base_of((0, 4)), entering, nothing, nothing, jnp.int32(0))
    spread = matmul(lax.all_gather(hidden, "seq", axis=0, tiled=True), w_out)
    partial_value = lax.all_to_all(spread, "seq", split_axis=0, concat_axis=1, tiled=True)
    summed = lax.psum_scatter(partial_value, "chan", scatter_dimension=1, tiled=True)
    return summed.astype(BF16)


def lined(base_of, hidden_of, state, w_out, fade, rows, index):
    depth = 4
    z, y = index // 2, index % 2

    def along(x, moves, name):
        return moved(x, "seq", [(a * 2 + b, c * 2 + b) for a, c in moves for b in range(2)], name)

    def across(x, planes, name):
        return moved(x, "seq", [(a * 2 + b, a * 2 + 1 - b) for a in planes for b in range(2)], name)

    def shift(by):
        return [(a, a + by) for a in range(depth) if 0 <= a + by < depth]

    every = range(depth)
    other = across(state, every, "state_y")
    other, base = fence(other, base_of((0, 2)))
    first = jnp.where(y == 0, state, other)
    second = jnp.where(y == 0, other, state)
    plane = first.astype(F32) * fade(rows) + second.astype(F32)
    below = along(plane.astype(BF16), shift(1), "state_1")
    below, base = fence(below, base_of((2, 3), base))
    two_below = (plane + below.astype(F32) * fade(2 * rows)).astype(BF16)
    further = along(two_below, shift(2), "state_2")
    base = base_of((3, 4), base)
    hidden = hidden_of(base, below, further, first, y)

    chan = lax.axis_index("chan")
    side, core = chan // 2, chan % 2
    pairwise = [(0, 1), (1, 0), (2, 3), (3, 2)]
    inner, outward = [(1, 2), (2, 1)], [(1, 0), (2, 3)]
    near_y = across(hidden, every, "near_y")
    one = along(hidden, pairwise, "one")
    middle = along(hidden, inner, "middle")
    one, middle, near_y = fence(one, middle, near_y)

    one_y = across(one, every, "one_y")
    given = along(one, inner, "given")
    out2 = along(middle, outward, "out2")
    given, out2, one_y, late_y = fence(given, out2, one_y, near_y[:, hidden.shape[1] // 2 :])

    at_end = z % 3 == 0
    two = jnp.where(at_end, out2, given)
    two_y = across(two, every, "two_y")
    out3 = along(given, outward, "out3")
    split = hidden.shape[1] // 2
    middle_y = along(late_y, inner, "middle_y")

    flip = [(c, c ^ 1) for c in range(4)]
    turn = [(c, c ^ 2) for c in range(4)]

    def root(group, a):
        return (a // 2) ^ (group % 2)

    def owners(group):
        return [
            [
                (
                    (a * 2 + b) * 4 + ((d ^ k) if group == 0 else root(group + g, a)) * 2 + (k if group == 0 else d),
                    ((a ^ (group + (k if group == 0 else g))) * 2 + (b ^ d)) * 4 + a,
                )
                for a in every
                for b in range(2)
                for k, g in (((0, 0), (1, 0)) if group == 0 else ((0, 0), (0, 1)))
            ]
            for d in range(2)
        ]

    even = [matmul(block, w_out) for block in (hidden, near_y)]
    odd = [matmul(block, w_out) for block in (one, one_y)]
    keep = jnp.stack([jnp.where(core == 0, a, b) for a, b in zip(even, odd)])
    send = jnp.stack([jnp.where(core == 0, b, a).astype(BF16) for a, b in zip(even, odd)])
    close_core = moved(send, "chan", flip, "core_0")
    keep = keep + close_core.astype(F32)
    send = jnp.where(side == core, keep[1], keep[0]).astype(BF16)
    keep = jnp.where(side == core, keep[0], keep[1])
    close_side = moved(send, "chan", turn, "side_0")

    def remote(group, parts, before):
        first, second = parts
        keep = jnp.where(core == 0, first, second)
        send = fence(jnp.where(core == 0, second, first).astype(BF16), *before)[0]
        keep = keep + moved(send, "chan", flip, f"core_{group}").astype(F32)
        pairs = [
            ((a * 2 + b) * 4 + (1 - root(group, a)) * 2 + k, (a * 2 + b) * 4 + root(group, a) * 2 + k)
            for a in every
            for b in range(2)
            for k in range(2)
        ]
        turned = moved(keep.astype(BF16), BOTH, pairs, f"side_{group}")
        return (keep + turned.astype(F32)).astype(BF16)

    out3, two_y, close_side, middle_y = fence(out3, two_y, close_side, middle_y)
    three = jnp.where(at_end, out3, middle)
    three_y = across(three[:, :split], every, "three_y")
    out_y = along(two_y[:, split:], outward, "out_y")
    with_three = matmul(three, w_out)
    tile = (keep + close_side.astype(F32)).astype(BF16)
    three_y, out_y, tile = fence(three_y, out_y, tile)
    close = [moved(tile, BOTH, pairs, "own_0") for pairs in owners(0)]
    with_three_y = matmul(three_y, w_out[:split]) + matmul(jnp.where(at_end, out_y, middle_y), w_out[split:])
    tile2 = remote(2, [matmul(two, w_out), matmul(two_y, w_out)], [with_three])
    with_three_y, tile2 = fence(with_three_y, tile2)
    tile3 = remote(3, [with_three, with_three_y], [])
    tile = jnp.where(side == root(2, z), tile2, tile3)
    far = [moved(tile, BOTH, pairs, "own_2") for pairs in owners(2)]
    near_here = (z ^ chan) < 2
    same = jnp.where(near_here, close[0], far[0])
    cross = jnp.where(near_here, close[1], far[1])
    low = jnp.where(y == 0, same, cross)
    high = jnp.where(y == 0, cross, same)
    return jnp.concatenate([low, high], axis=1)


def local(q_proj, k_proj, v_proj, residues, rates, skip_gain, w_out):
    rows, width = q_proj.shape
    parts = lax.axis_size("seq")
    index = lax.axis_index("seq")
    total = rows * parts
    modes = rates.shape[1]
    res_t, rate_t = residues.T, rates.T
    state = run(
        functools.partial(state_kernel, total),
        jax.ShapeDtypeStruct((modes, width), BF16),
        1,
        48,
        60,
        [k_proj, v_proj, rate_t],
    )

    def base_of(window, filled=None):
        return run(
            functools.partial(local_kernel, total),
            jax.ShapeDtypeStruct((rows, width), F32),
            2,
            100,
            60,
            [q_proj, k_proj, v_proj, res_t, rate_t, skip_gain[None, :]],
            window,
            filled,
        )

    def hidden_of(base, below, further, first, odd):
        return run(
            functools.partial(carry_kernel, total),
            jax.ShapeDtypeStruct((rows, width), BF16),
            1,
            32,
            16,
            [q_proj, base, below, further, first, res_t, rate_t],
            scalars=(odd.astype(jnp.int32)[None],),
        )

    def fade(steps):
        return jnp.exp(rate_t * (-float(steps) / total))

    if parts == 8 and lax.axis_size("chan") == 4:
        return lined(base_of, hidden_of, state, w_out, fade, rows, index)
    return general(base_of, hidden_of, state, w_out, fade, rows, index, parts)


def solution(mesh):
    return jax.shard_map(
        local,
        mesh=mesh,
        in_specs=(
            P("seq", "chan"),
            P("seq", "chan"),
            P("seq", "chan"),
            P("chan", None),
            P("chan", None),
            P("chan"),
            P("chan", "seq"),
        ),
        out_specs=P("seq", "chan"),
        check_vma=False,
    )
```

```python
import functools

import jax
import jax.numpy as jnp
from jax import lax
from jax.experimental import pallas as pl
from jax.experimental.pallas import tpu as pltpu
from jax.sharding import PartitionSpec as P

BF16 = jnp.bfloat16
F32 = jnp.float32
SUB = 8
LANES = 128
BOTH = ("seq", "chan")


def spread_rows(row):
    return jnp.broadcast_to(row, (SUB, row.shape[-1]))


def source_rows(k_ref, v_ref, x_ref, lanes):
    x_ref[...] = k_ref[:, lanes].astype(F32) * v_ref[:, lanes].astype(F32)
    length = x_ref.shape[0] // SUB
    return [x_ref[pl.ds(i, SUB, stride=length), :] for i in range(length)]


def state_kernel(total, k_ref, v_ref, rate_ref, state_ref, x_ref):
    modes, width = rate_ref.shape
    length = x_ref.shape[0] // SUB
    block = lax.broadcasted_iota(jnp.int32, (SUB, LANES), 0).astype(F32)

    @pl.loop(0, width // LANES)
    def _(chunk):
        lanes = pl.ds(pl.multiple_of(chunk * LANES, LANES), LANES)
        x = source_rows(k_ref, v_ref, x_ref, lanes)
        rate = rate_ref[:, lanes] * (-1.0 / total)
        decay = jnp.exp(rate)
        rows = []
        for m in range(modes):
            d = spread_rows(decay[m : m + 1])
            state = x[0]
            for i in range(1, length):
                state = state * d + x[i]
            weight = jnp.exp(spread_rows(rate[m : m + 1]) * ((SUB - 1.0 - block) * length))
            rows.append(jnp.sum(state * weight, axis=0, keepdims=True))
        state_ref[:, lanes] = jnp.concatenate(rows, axis=0).astype(BF16)


def local_kernel(total, q_ref, k_ref, v_ref, res_ref, rate_ref, skip_ref, *rest):
    base_ref, x_ref, y_ref = rest[-3:]
    modes, width = rate_ref.shape
    length = x_ref.shape[0] // SUB
    block = lax.broadcasted_iota(jnp.int32, (SUB, LANES), 0)

    @pl.loop(0, width // LANES)
    def _(chunk):
        lanes = pl.ds(pl.multiple_of(chunk * LANES, LANES), LANES)
        x = source_rows(k_ref, v_ref, x_ref, lanes)
        rate = rate_ref[:, lanes] * (-1.0 / total)
        gain = res_ref[:, lanes] * jnp.sqrt(rate_ref[:, lanes] * (2.0 / total))
        decay = jnp.exp(rate)
        y = [spread_rows(skip_ref[:, lanes]) * x[i] for i in range(length)]
        power = gain
        for j in range(length):
            tap = spread_rows(jnp.sum(power, axis=0, keepdims=True))
            for i in range(j, length):
                y[i] = y[i] + tap * x[i - j]
            power = power * decay
        for m in range(modes):
            d = spread_rows(decay[m : m + 1])
            state = x[0]
            for i in range(1, length):
                state = state * d + x[i]
            step = spread_rows(rate[m : m + 1]) * length
            state = jnp.where(block >= 1, pltpu.roll(state, 1, 0), 0.0)
            for shift in (1, 2, 4):
                moved = jnp.where(block >= shift, pltpu.roll(state, shift, 0), 0.0)
                state = state + jnp.exp(step * shift) * moved
            state = state * spread_rows(gain[m : m + 1])
            for i in range(length):
                state = state * d
                y[i] = y[i] + state
        for i in range(length):
            y_ref[pl.ds(i, SUB, stride=length), :] = y[i]
        base_ref[:, lanes] = y_ref[...] * q_ref[:, lanes].astype(F32)


def carry_kernel(total, odd_ref, q_ref, base_ref, below_ref, further_ref, first_ref, res_ref, rate_ref, out_ref, y_ref):
    modes, width = rate_ref.shape
    length = y_ref.shape[0] // SUB
    block = lax.broadcasted_iota(jnp.int32, (SUB, LANES), 0).astype(F32)

    @pl.loop(0, width // LANES)
    def _(chunk):
        lanes = pl.ds(pl.multiple_of(chunk * LANES, LANES), LANES)
        rate = rate_ref[:, lanes] * (-1.0 / total)
        rows = SUB * length
        start = below_ref[:, lanes].astype(F32) + further_ref[:, lanes].astype(F32) * jnp.exp(rate * (2 * rows))
        later = start * jnp.exp(rate * rows) + first_ref[:, lanes].astype(F32)
        start = jnp.where(odd_ref[0] == 1, later, start)
        start = start * res_ref[:, lanes] * jnp.sqrt(rate_ref[:, lanes] * (2.0 / total))
        decay = jnp.exp(rate)
        y = [jnp.zeros((SUB, LANES), F32) for i in range(length)]
        for m in range(modes):
            d = spread_rows(decay[m : m + 1])
            state = spread_rows(start[m : m + 1]) * jnp.exp(spread_rows(rate[m : m + 1]) * (block * length))
            for i in range(length):
                state = state * d
                y[i] = y[i] + state
        for i in range(length):
            y_ref[pl.ds(i, SUB, stride=length), :] = y[i]
        out_ref[:, lanes] = (base_ref[:, lanes] + y_ref[...] * q_ref[:, lanes].astype(F32)).astype(BF16)


def run(kernel, out, scratch, ops, mib, args, window=None, filled=None, scalars=()):
    rows, width = args[0].shape
    part = min(width // 4, 4 * LANES)
    steps = width // part
    first = 0
    if window is not None:
        first, steps = window[0] * steps // 4, (window[1] - window[0]) * steps // 4
    specs = [pl.BlockSpec(memory_space=pltpu.SMEM)] * len(scalars)
    specs += [pl.BlockSpec((arg.shape[0], part), lambda i: (0, i + first)) for arg in args]
    if filled is not None:
        specs.append(pl.BlockSpec(memory_space=pl.ANY))
    return pl.pallas_call(
        kernel,
        grid=(steps,),
        out_shape=out,
        in_specs=specs,
        out_specs=pl.BlockSpec((out.shape[0], part), lambda i: (0, i + first)),
        scratch_shapes=[pltpu.VMEM((rows, LANES), F32)] * scratch,
        input_output_aliases={} if filled is None else {len(specs) - 1: 0},
        compiler_params=pltpu.CompilerParams(vmem_limit_bytes=mib * 1024 * 1024),
        cost_estimate=pl.CostEstimate(
            flops=ops * rows * part * steps, bytes_accessed=6 * rows * part * steps, transcendentals=0
        ),
    )(*scalars, *args, *(() if filled is None else (filled,)))


def matmul(x, w):
    return jnp.dot(x, w, preferred_element_type=F32)


def moved(x, axes, pairs, name):
    with jax.named_scope(name):
        return lax.ppermute(x, axes, pairs)


def fence(*xs):
    return lax.optimization_barrier(xs)


def general(base_of, hidden_of, state, w_out, fade, rows, index, parts):
    states = lax.all_gather(state, "seq", axis=0)
    entering = jnp.zeros(state.shape, F32)
    for b in range(parts):
        entering = jnp.where(b < index, entering * fade(rows) + states[b].astype(F32), entering)
    nothing = jnp.zeros_like(state)
    hidden = hidden_of(base_of((0, 4)), entering, nothing, nothing, jnp.int32(0))
    spread = matmul(lax.all_gather(hidden, "seq", axis=0, tiled=True), w_out)
    partial_value = lax.all_to_all(spread, "seq", split_axis=0, concat_axis=1, tiled=True)
    summed = lax.psum_scatter(partial_value, "chan", scatter_dimension=1, tiled=True)
    return summed.astype(BF16)


def lined(base_of, hidden_of, state, w_out, fade, rows, index):
    depth = 4
    z, y = index // 2, index % 2

    def along(x, moves, name):
        return moved(x, "seq", [(a * 2 + b, c * 2 + b) for a, c in moves for b in range(2)], name)

    def across(x, planes, name):
        return moved(x, "seq", [(a * 2 + b, a * 2 + 1 - b) for a in planes for b in range(2)], name)

    def shift(by):
        return [(a, a + by) for a in range(depth) if 0 <= a + by < depth]

    every = range(depth)
    other = across(state, every, "state_y")
    other, base = fence(other, base_of((0, 2)))
    first = jnp.where(y == 0, state, other)
    second = jnp.where(y == 0, other, state)
    plane = first.astype(F32) * fade(rows) + second.astype(F32)
    below = along(plane.astype(BF16), shift(1), "state_1")
    below, base = fence(below, base_of((2, 3), base))
    two_below = (plane + below.astype(F32) * fade(2 * rows)).astype(BF16)
    further = along(two_below, shift(2), "state_2")
    base = base_of((3, 4), base)
    hidden = hidden_of(base, below, further, first, y)

    chan = lax.axis_index("chan")
    side, core = chan // 2, chan % 2
    pairwise = [(0, 1), (1, 0), (2, 3), (3, 2)]
    inner, outward = [(1, 2), (2, 1)], [(1, 0), (2, 3)]
    near_y = across(hidden, every, "near_y")
    one = along(hidden, pairwise, "one")
    middle = along(hidden, inner, "middle")
    one, middle, near_y = fence(one, middle, near_y)

    one_y = across(one, every, "one_y")
    given = along(one, inner, "given")
    out2 = along(middle, outward, "out2")
    given, out2, one_y, late_y = fence(given, out2, one_y, near_y[:, hidden.shape[1] // 2 :])

    at_end = z % 3 == 0
    two = jnp.where(at_end, out2, given)
    two_y = across(two, every, "two_y")
    out3 = along(given, outward, "out3")
    split = hidden.shape[1] // 2
    middle_y = along(late_y, inner, "middle_y")

    flip = [(c, c ^ 1) for c in range(4)]
    turn = [(c, c ^ 2) for c in range(4)]

    def root(group, a):
        return (a // 2) ^ (group % 2)

    def owners(group):
        return [
            [
                (
                    (a * 2 + b) * 4 + ((d ^ k) if group == 0 else root(group + g, a)) * 2 + (k if group == 0 else d),
                    ((a ^ (group + (k if group == 0 else g))) * 2 + (b ^ d)) * 4 + a,
                )
                for a in every
                for b in range(2)
                for k, g in (((0, 0), (1, 0)) if group == 0 else ((0, 0), (0, 1)))
            ]
            for d in range(2)
        ]

    even = [matmul(block, w_out) for block in (hidden, near_y)]
    odd = [matmul(block, w_out) for block in (one, one_y)]
    keep = jnp.stack([jnp.where(core == 0, a, b) for a, b in zip(even, odd)])
    send = jnp.stack([jnp.where(core == 0, b, a).astype(BF16) for a, b in zip(even, odd)])
    close_core = moved(send, "chan", flip, "core_0")
    keep = keep + close_core.astype(F32)
    send = jnp.where(side == core, keep[1], keep[0]).astype(BF16)
    keep = jnp.where(side == core, keep[0], keep[1])
    close_side = moved(send, "chan", turn, "side_0")

    def remote(group, parts, before):
        first, second = parts
        keep = jnp.where(core == 0, first, second)
        send = fence(jnp.where(core == 0, second, first).astype(BF16), *before)[0]
        keep = keep + moved(send, "chan", flip, f"core_{group}").astype(F32)
        pairs = [
            ((a * 2 + b) * 4 + (1 - root(group, a)) * 2 + k, (a * 2 + b) * 4 + root(group, a) * 2 + k)
            for a in every
            for b in range(2)
            for k in range(2)
        ]
        turned = moved(keep.astype(BF16), BOTH, pairs, f"side_{group}")
        return (keep + turned.astype(F32)).astype(BF16)

    out3, two_y, middle_y = fence(out3, two_y, middle_y)
    three = jnp.where(at_end, out3, middle)
    three_y = across(three[:, :split], every, "three_y")
    out_y = along(two_y[:, split:], outward, "out_y")
    with_three = matmul(three, w_out)
    three_y, out_y, close_side = fence(three_y, out_y, close_side)
    tile = (keep + close_side.astype(F32)).astype(BF16)
    close = [moved(tile, BOTH, pairs, "own_0") for pairs in owners(0)]
    with_three_y = matmul(three_y, w_out[:split]) + matmul(jnp.where(at_end, out_y, middle_y), w_out[split:])
    tile2 = remote(2, [matmul(two, w_out), matmul(two_y, w_out)], [with_three])
    with_three_y, tile2 = fence(with_three_y, tile2)
    tile3 = remote(3, [with_three, with_three_y], [])
    tile = jnp.where(side == root(2, z), tile2, tile3)
    far = [moved(tile, BOTH, pairs, "own_2") for pairs in owners(2)]
    near_here = (z ^ chan) < 2
    same = jnp.where(near_here, close[0], far[0])
    cross = jnp.where(near_here, close[1], far[1])
    low = jnp.where(y == 0, same, cross)
    high = jnp.where(y == 0, cross, same)
    return jnp.concatenate([low, high], axis=1)


def local(q_proj, k_proj, v_proj, residues, rates, skip_gain, w_out):
    rows, width = q_proj.shape
    parts = lax.axis_size("seq")
    index = lax.axis_index("seq")
    total = rows * parts
    modes = rates.shape[1]
    res_t, rate_t = residues.T, rates.T
    state = run(
        functools.partial(state_kernel, total),
        jax.ShapeDtypeStruct((modes, width), BF16),
        1,
        48,
        60,
        [k_proj, v_proj, rate_t],
    )

    def base_of(window, filled=None):
        return run(
            functools.partial(local_kernel, total),
            jax.ShapeDtypeStruct((rows, width), F32),
            2,
            100,
            60,
            [q_proj, k_proj, v_proj, res_t, rate_t, skip_gain[None, :]],
            window,
            filled,
        )

    def hidden_of(base, below, further, first, odd):
        return run(
            functools.partial(carry_kernel, total),
            jax.ShapeDtypeStruct((rows, width), BF16),
            1,
            32,
            16,
            [q_proj, base, below, further, first, res_t, rate_t],
            scalars=(odd.astype(jnp.int32)[None],),
        )

    def fade(steps):
        return jnp.exp(rate_t * (-float(steps) / total))

    if parts == 8 and lax.axis_size("chan") == 4:
        return lined(base_of, hidden_of, state, w_out, fade, rows, index)
    return general(base_of, hidden_of, state, w_out, fade, rows, index, parts)


def solution(mesh):
    return jax.shard_map(
        local,
        mesh=mesh,
        in_specs=(
            P("seq", "chan"),
            P("seq", "chan"),
            P("seq", "chan"),
            P("chan", None),
            P("chan", None),
            P("chan"),
            P("chan", "seq"),
        ),
        out_specs=P("seq", "chan"),
        check_vma=False,
    )
```

```python
import functools
import itertools

import jax
import jax.numpy as jnp
from jax import lax
from jax.experimental import pallas as pl
from jax.experimental.pallas import tpu as pltpu
from jax.sharding import PartitionSpec as P

BF16 = jnp.bfloat16
F32 = jnp.float32
SUB = 8
LANES = 128
BOTH = ("seq", "chan")


def spread_rows(row):
    return jnp.broadcast_to(row, (SUB, row.shape[-1]))


def source_rows(k_ref, v_ref, x_ref, lanes):
    x_ref[...] = k_ref[:, lanes].astype(F32) * v_ref[:, lanes].astype(F32)
    length = x_ref.shape[0] // SUB
    return [x_ref[pl.ds(i, SUB, stride=length), :] for i in range(length)]


def state_kernel(total, k_ref, v_ref, rate_ref, state_ref, x_ref):
    modes, width = rate_ref.shape
    length = x_ref.shape[0] // SUB
    block = lax.broadcasted_iota(jnp.int32, (SUB, LANES), 0).astype(F32)

    @pl.loop(0, width // LANES)
    def _(chunk):
        lanes = pl.ds(pl.multiple_of(chunk * LANES, LANES), LANES)
        x = source_rows(k_ref, v_ref, x_ref, lanes)
        rate = rate_ref[:, lanes] * (-1.0 / total)
        decay = jnp.exp(rate)
        rows = []
        for m in range(modes):
            d = spread_rows(decay[m : m + 1])
            state = x[0]
            for i in range(1, length):
                state = state * d + x[i]
            weight = jnp.exp(spread_rows(rate[m : m + 1]) * ((SUB - 1.0 - block) * length))
            rows.append(jnp.sum(state * weight, axis=0, keepdims=True))
        state_ref[:, lanes] = jnp.concatenate(rows, axis=0).astype(BF16)


def local_kernel(total, q_ref, k_ref, v_ref, res_ref, rate_ref, skip_ref, *rest):
    base_ref, x_ref, y_ref = rest[-3:]
    modes, width = rate_ref.shape
    length = x_ref.shape[0] // SUB
    block = lax.broadcasted_iota(jnp.int32, (SUB, LANES), 0)

    @pl.loop(0, width // LANES)
    def _(chunk):
        lanes = pl.ds(pl.multiple_of(chunk * LANES, LANES), LANES)
        x = source_rows(k_ref, v_ref, x_ref, lanes)
        rate = rate_ref[:, lanes] * (-1.0 / total)
        gain = res_ref[:, lanes] * jnp.sqrt(rate_ref[:, lanes] * (2.0 / total))
        decay = jnp.exp(rate)
        y = [spread_rows(skip_ref[:, lanes]) * x[i] for i in range(length)]
        power = gain
        for j in range(length):
            tap = spread_rows(jnp.sum(power, axis=0, keepdims=True))
            for i in range(j, length):
                y[i] = y[i] + tap * x[i - j]
            power = power * decay
        for m in range(modes):
            d = spread_rows(decay[m : m + 1])
            state = x[0]
            for i in range(1, length):
                state = state * d + x[i]
            step = spread_rows(rate[m : m + 1]) * length
            state = jnp.where(block >= 1, pltpu.roll(state, 1, 0), 0.0)
            for shift in (1, 2, 4):
                moved = jnp.where(block >= shift, pltpu.roll(state, shift, 0), 0.0)
                state = state + jnp.exp(step * shift) * moved
            state = state * spread_rows(gain[m : m + 1])
            for i in range(length):
                state = state * d
                y[i] = y[i] + state
        for i in range(length):
            y_ref[pl.ds(i, SUB, stride=length), :] = y[i]
        base_ref[:, lanes] = y_ref[...] * q_ref[:, lanes].astype(F32)


def carry_kernel(total, odd_ref, q_ref, base_ref, below_ref, further_ref, first_ref, res_ref, rate_ref, out_ref, y_ref):
    modes, width = rate_ref.shape
    length = y_ref.shape[0] // SUB
    block = lax.broadcasted_iota(jnp.int32, (SUB, LANES), 0).astype(F32)

    @pl.loop(0, width // LANES)
    def _(chunk):
        lanes = pl.ds(pl.multiple_of(chunk * LANES, LANES), LANES)
        rate = rate_ref[:, lanes] * (-1.0 / total)
        rows = SUB * length
        start = below_ref[:, lanes].astype(F32) + further_ref[:, lanes].astype(F32) * jnp.exp(rate * (2 * rows))
        later = start * jnp.exp(rate * rows) + first_ref[:, lanes].astype(F32)
        start = jnp.where(odd_ref[0] == 1, later, start)
        start = start * res_ref[:, lanes] * jnp.sqrt(rate_ref[:, lanes] * (2.0 / total))
        decay = jnp.exp(rate)
        y = [jnp.zeros((SUB, LANES), F32) for i in range(length)]
        for m in range(modes):
            d = spread_rows(decay[m : m + 1])
            state = spread_rows(start[m : m + 1]) * jnp.exp(spread_rows(rate[m : m + 1]) * (block * length))
            for i in range(length):
                state = state * d
                y[i] = y[i] + state
        for i in range(length):
            y_ref[pl.ds(i, SUB, stride=length), :] = y[i]
        out_ref[:, lanes] = (base_ref[:, lanes] + y_ref[...] * q_ref[:, lanes].astype(F32)).astype(BF16)


def run(kernel, out, scratch, ops, mib, args, window=None, filled=None, scalars=()):
    rows, width = args[0].shape
    part = min(width // 4, 4 * LANES)
    steps = width // part
    first = 0
    if window is not None:
        first, steps = window[0] * steps // 4, (window[1] - window[0]) * steps // 4
    specs = [pl.BlockSpec(memory_space=pltpu.SMEM)] * len(scalars)
    specs += [pl.BlockSpec((arg.shape[0], part), lambda i: (0, i + first)) for arg in args]
    if filled is not None:
        specs.append(pl.BlockSpec(memory_space=pl.ANY))
    return pl.pallas_call(
        kernel,
        grid=(steps,),
        out_shape=out,
        in_specs=specs,
        out_specs=pl.BlockSpec((out.shape[0], part), lambda i: (0, i + first)),
        scratch_shapes=[pltpu.VMEM((rows, LANES), F32)] * scratch,
        input_output_aliases={} if filled is None else {len(specs) - 1: 0},
        compiler_params=pltpu.CompilerParams(vmem_limit_bytes=mib * 1024 * 1024),
        cost_estimate=pl.CostEstimate(
            flops=ops * rows * part * steps, bytes_accessed=6 * rows * part * steps, transcendentals=0
        ),
    )(*scalars, *args, *(() if filled is None else (filled,)))


def matmul(x, w):
    return jnp.dot(x, w, preferred_element_type=F32)


def moved(x, axes, pairs, name):
    with jax.named_scope(name):
        return lax.ppermute(x, axes, pairs)


def fence(*xs):
    return lax.optimization_barrier(xs)


def general(base_of, hidden_of, state, w_out, fade, rows, index, parts):
    states = lax.all_gather(state, "seq", axis=0)
    entering = jnp.zeros(state.shape, F32)
    for b in range(parts):
        entering = jnp.where(b < index, entering * fade(rows) + states[b].astype(F32), entering)
    nothing = jnp.zeros_like(state)
    hidden = hidden_of(base_of((0, 4)), entering, nothing, nothing, jnp.int32(0))
    spread = matmul(lax.all_gather(hidden, "seq", axis=0, tiled=True), w_out)
    partial_value = lax.all_to_all(spread, "seq", split_axis=0, concat_axis=1, tiled=True)
    summed = lax.psum_scatter(partial_value, "chan", scatter_dimension=1, tiled=True)
    return summed.astype(BF16)


def lined(base_of, hidden_of, state, w_out, fade, rows, index):
    depth = 4
    z, y = index // 2, index % 2

    def along(x, moves, name):
        return moved(x, "seq", [(a * 2 + b, c * 2 + b) for a, c in moves for b in range(2)], name)

    def across(x, planes, name):
        return moved(x, "seq", [(a * 2 + b, a * 2 + 1 - b) for a in planes for b in range(2)], name)

    def shift(by):
        return [(a, a + by) for a in range(depth) if 0 <= a + by < depth]

    every = range(depth)
    other = across(state, every, "state_y")
    other, base = fence(other, base_of((0, 2)))
    first = jnp.where(y == 0, state, other)
    second = jnp.where(y == 0, other, state)
    plane = first.astype(F32) * fade(rows) + second.astype(F32)
    below = along(plane.astype(BF16), shift(1), "state_1")
    below, base = fence(below, base_of((2, 3), base))
    two_below = (plane + below.astype(F32) * fade(2 * rows)).astype(BF16)
    further = along(two_below, shift(2), "state_2")
    base = base_of((3, 4), base)
    hidden = hidden_of(base, below, further, first, y)

    chan = lax.axis_index("chan")
    side, core = chan // 2, chan % 2
    pairwise = [(0, 1), (1, 0), (2, 3), (3, 2)]
    inner, outward = [(1, 2), (2, 1)], [(1, 0), (2, 3)]
    near_y = across(hidden, every, "near_y")
    one = along(hidden, pairwise, "one")
    middle = along(hidden, inner, "middle")
    one, middle, near_y = fence(one, middle, near_y)

    one_y = across(one, every, "one_y")
    given = along(one, inner, "given")
    out2 = along(middle, outward, "out2")
    given, out2, one_y, late_y = fence(given, out2, one_y, near_y[:, hidden.shape[1] // 2 :])

    at_end = z % 3 == 0
    two = jnp.where(at_end, out2, given)
    two_y = across(two, every, "two_y")
    out3 = along(given, outward, "out3")
    split = hidden.shape[1] // 2
    middle_y = along(late_y, inner, "middle_y")

    flip = [(c, c ^ 1) for c in range(4)]
    turn = [(c, c ^ 2) for c in range(4)]

    def owned(dy):
        pairs = []
        for a, b, x in itertools.product(every, range(2), range(2)):
            for k in range(2):
                apart = 2 + (x ^ (a // 2)) if k == dy else x
                pairs.append(((a * 2 + b) * 4 + x * 2 + k, ((a ^ apart) * 2 + (b ^ dy)) * 4 + a))
        return pairs

    def turned(here, first, second, pairs, name):
        keep = jnp.where(here, first, second)
        return keep, moved(jnp.where(here, second, first).astype(BF16), "chan", pairs, name)

    def far(first, second, dy):
        parts = jnp.stack([first, second])
        parts = parts + moved(parts.astype(BF16), "chan", [(1 - dy, dy), (3 - dy, 2 + dy)], f"core_far{dy}").astype(F32)
        return turned(side == z // 2, parts[0], parts[1], [(dy, 2 + dy), (2 + dy, dy)], f"side_far{dy}")

    ready = [[matmul(x, w_out) for x in (hidden, near_y)], [matmul(x, w_out) for x in (one, one_y)]]
    keep = jnp.stack([jnp.where(core == 0, second, first) for first, second in ready])
    send = jnp.stack([jnp.where(core == 0, first, second).astype(BF16) for first, second in ready])
    close = keep + moved(send, "chan", flip, "core_close").astype(F32)
    close_keep, close_side = turned(side == 0, close[0], close[1], turn, "side_close")

    out3, two_y, middle_y = fence(out3, two_y, middle_y)
    three = jnp.where(at_end, out3, middle)
    three_y = across(three[:, :split], every, "three_y")
    out_y = along(two_y[:, split:], outward, "out_y")
    with_three = matmul(three, w_out)
    far_keep, far_side = far(matmul(two, w_out), with_three, 0)
    three_y, out_y, close_side, far_side = fence(three_y, out_y, close_side, far_side)
    close_tile = (close_keep + close_side.astype(F32)).astype(BF16)
    tile = (far_keep + far_side.astype(F32)).astype(BF16)
    same = moved(jnp.where(core == 0, tile, close_tile), BOTH, owned(0), "own_0")
    with_three_y = matmul(three_y, w_out[:split]) + matmul(jnp.where(at_end, out_y, middle_y), w_out[split:])
    far_keep, far_side = far(matmul(two_y, w_out), with_three_y, 1)
    tile = (far_keep + far_side.astype(F32)).astype(BF16)
    cross = moved(jnp.where(core == 1, tile, close_tile), BOTH, owned(1), "own_1")
    low = jnp.where(y == 0, same, cross)
    high = jnp.where(y == 0, cross, same)
    return jnp.concatenate([low, high], axis=1)


def local(q_proj, k_proj, v_proj, residues, rates, skip_gain, w_out):
    rows, width = q_proj.shape
    parts = lax.axis_size("seq")
    index = lax.axis_index("seq")
    total = rows * parts
    modes = rates.shape[1]
    res_t, rate_t = residues.T, rates.T
    state = run(
        functools.partial(state_kernel, total),
        jax.ShapeDtypeStruct((modes, width), BF16),
        1,
        48,
        60,
        [k_proj, v_proj, rate_t],
    )

    def base_of(window, filled=None):
        return run(
            functools.partial(local_kernel, total),
            jax.ShapeDtypeStruct((rows, width), F32),
            2,
            100,
            60,
            [q_proj, k_proj, v_proj, res_t, rate_t, skip_gain[None, :]],
            window,
            filled,
        )

    def hidden_of(base, below, further, first, odd):
        return run(
            functools.partial(carry_kernel, total),
            jax.ShapeDtypeStruct((rows, width), BF16),
            1,
            32,
            16,
            [q_proj, base, below, further, first, res_t, rate_t],
            scalars=(odd.astype(jnp.int32)[None],),
        )

    def fade(steps):
        return jnp.exp(rate_t * (-float(steps) / total))

    if parts == 8 and lax.axis_size("chan") == 4:
        return lined(base_of, hidden_of, state, w_out, fade, rows, index)
    return general(base_of, hidden_of, state, w_out, fade, rows, index, parts)


def solution(mesh):
    return jax.shard_map(
        local,
        mesh=mesh,
        in_specs=(
            P("seq", "chan"),
            P("seq", "chan"),
            P("seq", "chan"),
            P("chan", None),
            P("chan", None),
            P("chan"),
            P("chan", "seq"),
        ),
        out_specs=P("seq", "chan"),
        check_vma=False,
    )
```

```python
import functools
import itertools

import jax
import jax.numpy as jnp
from jax import lax
from jax.experimental import pallas as pl
from jax.experimental.pallas import tpu as pltpu
from jax.sharding import PartitionSpec as P

BF16 = jnp.bfloat16
F32 = jnp.float32
SUB = 8
LANES = 128
BOTH = ("seq", "chan")


def spread_rows(row):
    return jnp.broadcast_to(row, (SUB, row.shape[-1]))


def runs(ref, chunk):
    length = ref.shape[1] // SUB
    return [ref[chunk, pl.ds(i, SUB, stride=length), :] for i in range(length)]


def powers(rate, length):
    once = jnp.exp(rate * length)
    twice = once * once
    return once, twice, twice * twice


def raised(steps, pows, m):
    result = jnp.where(steps % 2 == 1, spread_rows(pows[0][m : m + 1]), 1.0)
    result = result * jnp.where(steps // 2 % 2 == 1, spread_rows(pows[1][m : m + 1]), 1.0)
    return result * jnp.where(steps >= 4, spread_rows(pows[2][m : m + 1]), 1.0)


def state_kernel(total, pieces, *refs):
    hbm, (state_ref, *near, k_ref, v_ref, sems) = refs[:6], refs[6:]
    x_ref, rate_ref, gain_ref, q_ref, skip_ref = near
    modes, width = rate_ref.shape
    length = x_ref.shape[1] // SUB
    part = width // pieces

    def copies(piece):
        lanes = pl.ds(piece * part, part)
        pairs = zip(hbm[:4], (k_ref, v_ref, rate_ref, gain_ref))
        return [
            pltpu.make_async_copy(src.at[:, lanes], dst.at[:, lanes], sems.at[piece, j])
            for j, (src, dst) in enumerate(pairs)
        ]

    whole = [pltpu.make_async_copy(src, dst, sems.at[pieces, j]) for j, (src, dst) in enumerate(zip(hbm[4:6], (q_ref, skip_ref)))]
    for piece in range(pieces):
        for copy in copies(piece):
            copy.start()
    for copy in whole:
        copy.start()
    left = SUB - 1 - lax.broadcasted_iota(jnp.int32, (SUB, LANES), 0)
    for piece in range(pieces):
        for copy in copies(piece):
            copy.wait()

        @pl.loop(0, part // LANES)
        def _(chunk):
            chunk = piece * (part // LANES) + chunk
            lanes = pl.ds(pl.multiple_of(chunk * LANES, LANES), LANES)
            x_ref[chunk] = k_ref[:, lanes].astype(F32) * v_ref[:, lanes].astype(F32)
            gain_ref[:, lanes] = gain_ref[:, lanes] * jnp.sqrt(rate_ref[:, lanes] * (2.0 / total))
            x = runs(x_ref, chunk)
            rate = rate_ref[:, lanes] * (-1.0 / total)
            decay = jnp.exp(rate)
            pows = powers(rate, length)
            rows = []
            for m in range(modes):
                d = spread_rows(decay[m : m + 1])
                state = x[0]
                for i in range(1, length):
                    state = state * d + x[i]
                rows.append(jnp.sum(state * raised(left, pows, m), axis=0, keepdims=True))
            state_ref[:, lanes] = jnp.concatenate(rows, axis=0).astype(BF16)

    for copy in whole:
        copy.wait()


def local_kernel(total, window, x_ref, rate_ref, gain_ref, skip_ref, *rest):
    base_ref = rest[-1]
    modes, width = rate_ref.shape
    length = x_ref.shape[1] // SUB
    block = lax.broadcasted_iota(jnp.int32, (SUB, LANES), 0)

    @pl.loop(window[0], window[1])
    def _(chunk):
        lanes = pl.ds(pl.multiple_of(chunk * LANES, LANES), LANES)
        x = runs(x_ref, chunk)
        rate = rate_ref[:, lanes] * (-1.0 / total)
        gain = gain_ref[:, lanes]
        decay = jnp.exp(rate)
        pows = powers(rate, length)
        y = [spread_rows(skip_ref[:, lanes]) * x[i] for i in range(length)]
        power = gain
        for j in range(length):
            tap = spread_rows(jnp.sum(power, axis=0, keepdims=True))
            for i in range(j, length):
                y[i] = y[i] + tap * x[i - j]
            power = power * decay
        for m in range(modes):
            d = spread_rows(decay[m : m + 1])
            state = x[0]
            for i in range(1, length):
                state = state * d + x[i]
            state = jnp.where(block >= 1, pltpu.roll(state, 1, 0), 0.0)
            for shift, step in zip((1, 2, 4), pows):
                moved_on = jnp.where(block >= shift, pltpu.roll(state, shift, 0), 0.0)
                state = state + spread_rows(step[m : m + 1]) * moved_on
            state = state * spread_rows(gain[m : m + 1])
            for i in range(length):
                state = state * d
                y[i] = y[i] + state
        for i in range(length):
            base_ref[chunk, pl.ds(i, SUB, stride=length), :] = y[i]


def carry_kernel(total, odd_ref, q_ref, base_ref, below_ref, further_ref, first_ref, rate_ref, gain_ref, out_ref, y_ref):
    modes, width = rate_ref.shape
    length = y_ref.shape[0] // SUB
    rows = y_ref.shape[0]
    block = lax.broadcasted_iota(jnp.int32, (SUB, LANES), 0)

    @pl.loop(0, width // LANES)
    def _(chunk):
        lanes = pl.ds(pl.multiple_of(chunk * LANES, LANES), LANES)
        rate = rate_ref[:, lanes] * (-1.0 / total)
        pows = powers(rate, length)
        start = below_ref[:, lanes].astype(F32) + further_ref[:, lanes].astype(F32) * jnp.exp(rate * (2 * rows))
        later = start * jnp.exp(rate * rows) + first_ref[:, lanes].astype(F32)
        start = jnp.where(odd_ref[0] == 1, later, start) * gain_ref[:, lanes]
        decay = jnp.exp(rate)
        y = runs(base_ref, chunk)
        for m in range(modes):
            d = spread_rows(decay[m : m + 1])
            state = spread_rows(start[m : m + 1]) * raised(block, pows, m)
            for i in range(length):
                state = state * d
                y[i] = y[i] + state
        for i in range(length):
            y_ref[pl.ds(i, SUB, stride=length), :] = y[i]
        out_ref[:, lanes] = (y_ref[...] * q_ref[:, lanes].astype(F32)).astype(BF16)


def run(kernel, outs, ops, mib, args, scratch=(), scalars=(), near=True, aliases={}):
    space = pltpu.VMEM if near else pl.ANY
    return pl.pallas_call(
        kernel,
        out_shape=[jax.ShapeDtypeStruct(shape, kind) for shape, kind in outs],
        in_specs=[pl.BlockSpec(memory_space=pltpu.SMEM)] * len(scalars)
        + [pl.BlockSpec(memory_space=space)] * len(args),
        out_specs=[pl.BlockSpec(memory_space=pltpu.VMEM)] * len(outs),
        scratch_shapes=scratch,
        input_output_aliases=aliases,
        compiler_params=pltpu.CompilerParams(vmem_limit_bytes=mib * 1024 * 1024),
        cost_estimate=pl.CostEstimate(
            flops=int(ops * args[0].size), bytes_accessed=4 * args[0].size, transcendentals=0
        ),
    )(*scalars, *args)


def matmul(x, w):
    return jnp.dot(x, w, preferred_element_type=F32)


def moved(x, axes, pairs, name):
    with jax.named_scope(name):
        return lax.ppermute(x, axes, pairs)


def fence(*xs):
    return lax.optimization_barrier(xs)


def general(base_of, hidden_of, state, w_out, fade, rows, index, parts):
    states = lax.all_gather(state, "seq", axis=0)
    entering = jnp.zeros(state.shape, F32)
    for b in range(parts):
        entering = jnp.where(b < index, entering * fade(rows) + states[b].astype(F32), entering)
    nothing = jnp.zeros_like(state)
    hidden = hidden_of(base_of((0, 16)), entering, nothing, nothing, jnp.int32(0))
    spread = matmul(lax.all_gather(hidden, "seq", axis=0, tiled=True), w_out)
    partial_value = lax.all_to_all(spread, "seq", split_axis=0, concat_axis=1, tiled=True)
    summed = lax.psum_scatter(partial_value, "chan", scatter_dimension=1, tiled=True)
    return summed.astype(BF16)


def lined(base_of, hidden_of, state, w_out, fade, rows, index):
    depth = 4
    z, y = index // 2, index % 2

    def along(x, moves, name):
        return moved(x, "seq", [(a * 2 + b, c * 2 + b) for a, c in moves for b in range(2)], name)

    def across(x, planes, name):
        return moved(x, "seq", [(a * 2 + b, a * 2 + 1 - b) for a in planes for b in range(2)], name)

    def shift(by):
        return [(a, a + by) for a in range(depth) if 0 <= a + by < depth]

    every = range(depth)
    other = across(state, every, "state_y")
    other, *base = fence(other, *base_of((0, 2)))
    first = jnp.where(y == 0, state, other)
    second = jnp.where(y == 0, other, state)
    plane = first.astype(F32) * fade(rows) + second.astype(F32)
    below = along(plane.astype(BF16), shift(1), "state_1")
    below, *base = fence(below, *base_of((2, 9), base))
    two_below = (plane + below.astype(F32) * fade(2 * rows)).astype(BF16)
    further = along(two_below, shift(2), "state_2")
    base = base_of((9, 16), base)
    hidden = hidden_of(base, below, further, first, y)

    chan = lax.axis_index("chan")
    side, core = chan // 2, chan % 2
    pairwise = [(0, 1), (1, 0), (2, 3), (3, 2)]
    inner, outward = [(1, 2), (2, 1)], [(1, 0), (2, 3)]
    near_y = across(hidden, every, "near_y")
    one = along(hidden, pairwise, "one")
    middle = along(hidden, inner, "middle")
    one, middle, near_y = fence(one, middle, near_y)

    one_y = across(one, every, "one_y")
    given = along(one, inner, "given")
    out2 = along(middle, outward, "out2")
    given, out2, one_y, late_y = fence(given, out2, one_y, near_y[:, hidden.shape[1] // 2 :])

    at_end = z % 3 == 0
    two = jnp.where(at_end, out2, given)
    two_y = across(two, every, "two_y")
    out3 = along(given, outward, "out3")
    split = hidden.shape[1] // 2
    middle_y = along(late_y, inner, "middle_y")

    flip = [(c, c ^ 1) for c in range(4)]
    turn = [(c, c ^ 2) for c in range(4)]

    def owned(dy):
        pairs = []
        for a, b, x in itertools.product(every, range(2), range(2)):
            for k in range(2):
                apart = 2 + (x ^ (a // 2)) if k == dy else x
                pairs.append(((a * 2 + b) * 4 + x * 2 + k, ((a ^ apart) * 2 + (b ^ dy)) * 4 + a))
        return pairs

    def turned(here, first, second, pairs, name):
        keep = jnp.where(here, first, second)
        return keep, moved(jnp.where(here, second, first).astype(BF16), "chan", pairs, name)

    def far(first, second, dy):
        parts = jnp.stack([first, second])
        parts = parts + moved(parts.astype(BF16), "chan", [(1 - dy, dy), (3 - dy, 2 + dy)], f"core_far{dy}").astype(F32)
        return turned(side == z // 2, parts[0], parts[1], [(dy, 2 + dy), (2 + dy, dy)], f"side_far{dy}")

    ready = [[matmul(x, w_out) for x in (hidden, near_y)], [matmul(x, w_out) for x in (one, one_y)]]
    keep = jnp.stack([jnp.where(core == 0, second, first) for first, second in ready])
    send = jnp.stack([jnp.where(core == 0, first, second).astype(BF16) for first, second in ready])
    close = keep + moved(send, "chan", flip, "core_close").astype(F32)
    close_keep, close_side = turned(side == 0, close[0], close[1], turn, "side_close")

    out3, two_y, middle_y = fence(out3, two_y, middle_y)
    three = jnp.where(at_end, out3, middle)
    three_y = across(three[:, :split], every, "three_y")
    out_y = along(two_y[:, split:], outward, "out_y")
    with_three = matmul(three, w_out)
    far_keep, far_side = far(matmul(two, w_out), with_three, 0)
    three_y, out_y, close_side, far_side = fence(three_y, out_y, close_side, far_side)
    close_tile = (close_keep + close_side.astype(F32)).astype(BF16)
    tile = (far_keep + far_side.astype(F32)).astype(BF16)
    same = moved(jnp.where(core == 0, tile, close_tile), BOTH, owned(0), "own_0")
    with_three_y = matmul(three_y, w_out[:split]) + matmul(jnp.where(at_end, out_y, middle_y), w_out[split:])
    far_keep, far_side = far(matmul(two_y, w_out), with_three_y, 1)
    tile = (far_keep + far_side.astype(F32)).astype(BF16)
    cross = moved(jnp.where(core == 1, tile, close_tile), BOTH, owned(1), "own_1")
    low = jnp.where(y == 0, same, cross)
    high = jnp.where(y == 0, cross, same)
    return jnp.concatenate([low, high], axis=1)


def local(q_proj, k_proj, v_proj, residues, rates, skip_gain, w_out):
    rows, width = q_proj.shape
    parts = lax.axis_size("seq")
    index = lax.axis_index("seq")
    total = rows * parts
    modes = rates.shape[1]
    res_t, rate_t = residues.T, rates.T
    pieces = 4
    tall, thin = (rows, width), (modes, width)
    chunks = (width // LANES, rows, LANES)
    state, x, rate_near, gain, q_near, skip = run(
        functools.partial(state_kernel, total, pieces),
        [(thin, BF16), (chunks, F32), (thin, F32), (thin, F32), (tall, BF16), ((1, width), F32)],
        48,
        60,
        [k_proj, v_proj, rate_t, res_t, q_proj, skip_gain[None, :]],
        [pltpu.VMEM(tall, BF16), pltpu.VMEM(tall, BF16), pltpu.SemaphoreType.DMA((pieces + 1, 4))],
        near=False,
    )

    def base_of(window, filled=()):
        count = width // LANES
        window = (window[0] * count // 16, window[1] * count // 16)
        return run(
            functools.partial(local_kernel, total, window),
            [(chunks, F32)],
            100 * (window[1] - window[0]) / count,
            16,
            [x, rate_near, gain, skip, *filled],
            aliases={4: 0} if filled else {},
        )

    def hidden_of(base, below, further, first, odd):
        return run(
            functools.partial(carry_kernel, total),
            [(tall, BF16)],
            32,
            16,
            [q_near, *base, below, further, first, rate_near, gain],
            [pltpu.VMEM((rows, LANES), F32)],
            scalars=(odd.astype(jnp.int32)[None],),
        )[0]

    def fade(steps):
        return jnp.exp(rate_t * (-float(steps) / total))

    if parts == 8 and lax.axis_size("chan") == 4:
        return lined(base_of, hidden_of, state, w_out, fade, rows, index)
    return general(base_of, hidden_of, state, w_out, fade, rows, index, parts)


def solution(mesh):
    return jax.shard_map(
        local,
        mesh=mesh,
        in_specs=(
            P("seq", "chan"),
            P("seq", "chan"),
            P("seq", "chan"),
            P("chan", None),
            P("chan", None),
            P("chan"),
            P("chan", "seq"),
        ),
        out_specs=P("seq", "chan"),
        check_vma=False,
    )
```

```python
import functools
import itertools

import jax
import jax.numpy as jnp
from jax import lax
from jax.experimental import pallas as pl
from jax.experimental.pallas import tpu as pltpu
from jax.sharding import PartitionSpec as P

BF16 = jnp.bfloat16
F32 = jnp.float32
SUB = 8
LANES = 128
BOTH = ("seq", "chan")


def spread_rows(row):
    return jnp.broadcast_to(row, (SUB, row.shape[-1]))


def runs(ref, chunk):
    length = ref.shape[1] // SUB
    return [ref[chunk, pl.ds(i, SUB, stride=length), :] for i in range(length)]


def powers(rate, length):
    once = jnp.exp(rate * length)
    twice = once * once
    return once, twice, twice * twice


def raised(steps, pows, m):
    result = jnp.where(steps % 2 == 1, spread_rows(pows[0][m : m + 1]), 1.0)
    result = result * jnp.where(steps // 2 % 2 == 1, spread_rows(pows[1][m : m + 1]), 1.0)
    return result * jnp.where(steps >= 4, spread_rows(pows[2][m : m + 1]), 1.0)


def state_kernel(total, pieces, *refs):
    hbm, (state_ref, *near, k_ref, v_ref, sems) = refs[:6], refs[6:]
    x_ref, rate_ref, gain_ref, q_ref, skip_ref = near
    modes, width = rate_ref.shape
    length = x_ref.shape[1] // SUB
    part = width // pieces

    def copies(piece):
        lanes = pl.ds(piece * part, part)
        pairs = zip(hbm[:4], (k_ref, v_ref, rate_ref, gain_ref))
        return [
            pltpu.make_async_copy(src.at[:, lanes], dst.at[:, lanes], sems.at[piece, j])
            for j, (src, dst) in enumerate(pairs)
        ]

    whole = [pltpu.make_async_copy(src, dst, sems.at[pieces, j]) for j, (src, dst) in enumerate(zip(hbm[4:6], (q_ref, skip_ref)))]
    for piece in range(pieces):
        for copy in copies(piece):
            copy.start()
    for copy in whole:
        copy.start()
    left = SUB - 1 - lax.broadcasted_iota(jnp.int32, (SUB, LANES), 0)
    for piece in range(pieces):
        for copy in copies(piece):
            copy.wait()

        @pl.loop(0, part // LANES)
        def _(chunk):
            chunk = piece * (part // LANES) + chunk
            lanes = pl.ds(pl.multiple_of(chunk * LANES, LANES), LANES)
            x_ref[chunk] = k_ref[:, lanes].astype(F32) * v_ref[:, lanes].astype(F32)
            gain_ref[:, lanes] = gain_ref[:, lanes] * jnp.sqrt(rate_ref[:, lanes] * (2.0 / total))
            x = runs(x_ref, chunk)
            rate = rate_ref[:, lanes] * (-1.0 / total)
            decay = jnp.exp(rate)
            pows = powers(rate, length)
            rows = []
            for m in range(modes):
                d = spread_rows(decay[m : m + 1])
                state = x[0]
                for i in range(1, length):
                    state = state * d + x[i]
                rows.append(jnp.sum(state * raised(left, pows, m), axis=0, keepdims=True))
            state_ref[:, lanes] = jnp.concatenate(rows, axis=0).astype(BF16)

    for copy in whole:
        copy.wait()


def local_kernel(total, window, x_ref, rate_ref, gain_ref, skip_ref, *rest):
    base_ref = rest[-1]
    modes, width = rate_ref.shape
    length = x_ref.shape[1] // SUB
    block = lax.broadcasted_iota(jnp.int32, (SUB, LANES), 0)

    @pl.loop(window[0], window[1])
    def _(chunk):
        lanes = pl.ds(pl.multiple_of(chunk * LANES, LANES), LANES)
        x = runs(x_ref, chunk)
        rate = rate_ref[:, lanes] * (-1.0 / total)
        gain = gain_ref[:, lanes]
        decay = jnp.exp(rate)
        pows = powers(rate, length)
        y = [spread_rows(skip_ref[:, lanes]) * x[i] for i in range(length)]
        power = gain
        for j in range(length):
            tap = spread_rows(jnp.sum(power, axis=0, keepdims=True))
            for i in range(j, length):
                y[i] = y[i] + tap * x[i - j]
            power = power * decay
        for m in range(modes):
            d = spread_rows(decay[m : m + 1])
            state = x[0]
            for i in range(1, length):
                state = state * d + x[i]
            state = jnp.where(block >= 1, pltpu.roll(state, 1, 0), 0.0)
            for shift, step in zip((1, 2, 4), pows):
                moved_on = jnp.where(block >= shift, pltpu.roll(state, shift, 0), 0.0)
                state = state + spread_rows(step[m : m + 1]) * moved_on
            state = state * spread_rows(gain[m : m + 1])
            for i in range(length):
                state = state * d
                y[i] = y[i] + state
        for i in range(length):
            base_ref[chunk, pl.ds(i, SUB, stride=length), :] = y[i]


def carry_kernel(total, odd_ref, q_ref, base_ref, below_ref, further_ref, first_ref, rate_ref, gain_ref, out_ref, y_ref):
    modes, width = rate_ref.shape
    length = y_ref.shape[0] // SUB
    rows = y_ref.shape[0]
    block = lax.broadcasted_iota(jnp.int32, (SUB, LANES), 0)

    @pl.loop(0, width // LANES)
    def _(chunk):
        lanes = pl.ds(pl.multiple_of(chunk * LANES, LANES), LANES)
        rate = rate_ref[:, lanes] * (-1.0 / total)
        pows = powers(rate, length)
        start = below_ref[:, lanes].astype(F32) + further_ref[:, lanes].astype(F32) * jnp.exp(rate * (2 * rows))
        later = start * jnp.exp(rate * rows) + first_ref[:, lanes].astype(F32)
        start = jnp.where(odd_ref[0] == 1, later, start) * gain_ref[:, lanes]
        decay = jnp.exp(rate)
        y = runs(base_ref, chunk)
        for m in range(modes):
            d = spread_rows(decay[m : m + 1])
            state = spread_rows(start[m : m + 1]) * raised(block, pows, m)
            for i in range(length):
                state = state * d
                y[i] = y[i] + state
        for i in range(length):
            y_ref[pl.ds(i, SUB, stride=length), :] = y[i]
        out_ref[:, lanes] = (y_ref[...] * q_ref[:, lanes].astype(F32)).astype(BF16)


def run(kernel, outs, ops, mib, args, scratch=(), scalars=(), near=True, aliases={}):
    space = pltpu.VMEM if near else pl.ANY
    return pl.pallas_call(
        kernel,
        out_shape=[jax.ShapeDtypeStruct(shape, kind) for shape, kind in outs],
        in_specs=[pl.BlockSpec(memory_space=pltpu.SMEM)] * len(scalars)
        + [pl.BlockSpec(memory_space=space)] * len(args),
        out_specs=[pl.BlockSpec(memory_space=pltpu.VMEM)] * len(outs),
        scratch_shapes=scratch,
        input_output_aliases=aliases,
        compiler_params=pltpu.CompilerParams(vmem_limit_bytes=mib * 1024 * 1024),
        cost_estimate=pl.CostEstimate(
            flops=int(ops * args[0].size), bytes_accessed=4 * args[0].size, transcendentals=0
        ),
    )(*scalars, *args)


def matmul(x, w):
    return jnp.dot(x, w, preferred_element_type=F32)


def moved(x, axes, pairs, name):
    with jax.named_scope(name):
        return lax.ppermute(x, axes, pairs)


def fence(*xs):
    return lax.optimization_barrier(xs)


def general(base_of, hidden_of, state, w_out, fade, rows, index, parts):
    states = lax.all_gather(state, "seq", axis=0)
    entering = jnp.zeros(state.shape, F32)
    for b in range(parts):
        entering = jnp.where(b < index, entering * fade(rows) + states[b].astype(F32), entering)
    nothing = jnp.zeros_like(state)
    hidden = hidden_of(base_of((0, 16)), entering, nothing, nothing, jnp.int32(0))
    spread = matmul(lax.all_gather(hidden, "seq", axis=0, tiled=True), w_out)
    partial_value = lax.all_to_all(spread, "seq", split_axis=0, concat_axis=1, tiled=True)
    summed = lax.psum_scatter(partial_value, "chan", scatter_dimension=1, tiled=True)
    return summed.astype(BF16)


def lined(base_of, hidden_of, state, w_out, fade, rows, index):
    depth = 4
    z, y = index // 2, index % 2

    def along(x, moves, name):
        return moved(x, "seq", [(a * 2 + b, c * 2 + b) for a, c in moves for b in range(2)], name)

    def across(x, planes, name):
        return moved(x, "seq", [(a * 2 + b, a * 2 + 1 - b) for a in planes for b in range(2)], name)

    def shift(by):
        return [(a, a + by) for a in range(depth) if 0 <= a + by < depth]

    every = range(depth)
    other = across(state, every, "state_y")
    other, *base = fence(other, *base_of((0, 2)))
    first = jnp.where(y == 0, state, other)
    second = jnp.where(y == 0, other, state)
    plane = first.astype(F32) * fade(rows) + second.astype(F32)
    below = along(plane.astype(BF16), shift(1), "state_1")
    below, *base = fence(below, *base_of((2, 9), base))
    two_below = (plane + below.astype(F32) * fade(2 * rows)).astype(BF16)
    further = along(two_below, shift(2), "state_2")
    base = base_of((9, 16), base)
    hidden = hidden_of(base, below, further, first, y)

    chan = lax.axis_index("chan")
    side, core = chan // 2, chan % 2
    pairwise = [(0, 1), (1, 0), (2, 3), (3, 2)]
    inner, outward = [(1, 2), (2, 1)], [(1, 0), (2, 3)]
    near_y = across(hidden, every, "near_y")
    one = along(hidden, pairwise, "one")
    middle = along(hidden, inner, "middle")
    one, middle, near_y = fence(one, middle, near_y)

    one_y = across(one, every, "one_y")
    given = along(one, inner, "given")
    out2 = along(middle, outward, "out2")
    given, out2, one_y, late_y = fence(given, out2, one_y, near_y[:, hidden.shape[1] // 2 :])

    at_end = z % 3 == 0
    two = jnp.where(at_end, out2, given)
    two_y = across(two, every, "two_y")
    out3 = along(given, outward, "out3")
    split = hidden.shape[1] // 2
    middle_y = along(late_y, inner, "middle_y")

    flip = [(c, c ^ 1) for c in range(4)]
    turn = [(c, c ^ 2) for c in range(4)]

    def owned(dy):
        pairs = []
        for a, b, x in itertools.product(every, range(2), range(2)):
            for k in range(2):
                apart = 2 + (x ^ (a // 2)) if k == dy else x
                pairs.append(((a * 2 + b) * 4 + x * 2 + k, ((a ^ apart) * 2 + (b ^ dy)) * 4 + a))
        return pairs

    def turned(here, first, second, pairs, name):
        keep = jnp.where(here, first, second)
        return keep, moved(jnp.where(here, second, first).astype(BF16), "chan", pairs, name)

    def far(first, second, dy):
        parts = jnp.stack([first.astype(BF16), second.astype(BF16)])
        given = moved(parts, "chan", [(1 - dy, dy), (3 - dy, 2 + dy)], f"core_far{dy}")
        parts = (parts.astype(F32) + given.astype(F32)).astype(BF16)
        return turned(side == z // 2, parts[0], parts[1], [(dy, 2 + dy), (2 + dy, dy)], f"side_far{dy}")

    ready = [[matmul(x, w_out) for x in (hidden, near_y)], [matmul(x, w_out) for x in (one, one_y)]]
    keep = jnp.stack([jnp.where(core == 0, second, first) for first, second in ready])
    send = jnp.stack([jnp.where(core == 0, first, second).astype(BF16) for first, second in ready])
    close = keep + moved(send, "chan", flip, "core_close").astype(F32)
    close_keep, close_side = turned(side == 0, close[0], close[1], turn, "side_close")

    out3, two_y, middle_y = fence(out3, two_y, middle_y)
    three = jnp.where(at_end, out3, middle)
    three_y = across(three[:, :split], every, "three_y")
    out_y = along(two_y[:, split:], outward, "out_y")
    with_three = matmul(three, w_out)
    far_keep, far_side = far(matmul(two, w_out), with_three, 0)
    three_y, out_y, close_side, far_side = fence(three_y, out_y, close_side, far_side)
    close_tile = (close_keep + close_side.astype(F32)).astype(BF16)
    tile = (far_keep.astype(F32) + far_side.astype(F32)).astype(BF16)
    same = moved(jnp.where(core == 0, tile, close_tile), BOTH, owned(0), "own_0")
    with_three_y = matmul(three_y, w_out[:split]) + matmul(jnp.where(at_end, out_y, middle_y), w_out[split:])
    far_keep, far_side = far(matmul(two_y, w_out), with_three_y, 1)
    tile = (far_keep.astype(F32) + far_side.astype(F32)).astype(BF16)
    cross = moved(jnp.where(core == 1, tile, close_tile), BOTH, owned(1), "own_1")
    low = jnp.where(y == 0, same, cross)
    high = jnp.where(y == 0, cross, same)
    return jnp.concatenate([low, high], axis=1)


def local(q_proj, k_proj, v_proj, residues, rates, skip_gain, w_out):
    rows, width = q_proj.shape
    parts = lax.axis_size("seq")
    index = lax.axis_index("seq")
    total = rows * parts
    modes = rates.shape[1]
    res_t, rate_t = residues.T, rates.T
    pieces = 4
    tall, thin = (rows, width), (modes, width)
    chunks = (width // LANES, rows, LANES)
    state, x, rate_near, gain, q_near, skip = run(
        functools.partial(state_kernel, total, pieces),
        [(thin, BF16), (chunks, F32), (thin, F32), (thin, F32), (tall, BF16), ((1, width), F32)],
        48,
        60,
        [k_proj, v_proj, rate_t, res_t, q_proj, skip_gain[None, :]],
        [pltpu.VMEM(tall, BF16), pltpu.VMEM(tall, BF16), pltpu.SemaphoreType.DMA((pieces + 1, 4))],
        near=False,
    )

    def base_of(window, filled=()):
        count = width // LANES
        window = (window[0] * count // 16, window[1] * count // 16)
        return run(
            functools.partial(local_kernel, total, window),
            [(chunks, F32)],
            100 * (window[1] - window[0]) / count,
            16,
            [x, rate_near, gain, skip, *filled],
            aliases={4: 0} if filled else {},
        )

    def hidden_of(base, below, further, first, odd):
        return run(
            functools.partial(carry_kernel, total),
            [(tall, BF16)],
            32,
            16,
            [q_near, *base, below, further, first, rate_near, gain],
            [pltpu.VMEM((rows, LANES), F32)],
            scalars=(odd.astype(jnp.int32)[None],),
        )[0]

    def fade(steps):
        return jnp.exp(rate_t * (-float(steps) / total))

    if parts == 8 and lax.axis_size("chan") == 4:
        return lined(base_of, hidden_of, state, w_out, fade, rows, index)
    return general(base_of, hidden_of, state, w_out, fade, rows, index, parts)


def solution(mesh):
    return jax.shard_map(
        local,
        mesh=mesh,
        in_specs=(
            P("seq", "chan"),
            P("seq", "chan"),
            P("seq", "chan"),
            P("chan", None),
            P("chan", None),
            P("chan"),
            P("chan", "seq"),
        ),
        out_specs=P("seq", "chan"),
        check_vma=False,
    )
```

```python
import functools
import itertools

import jax
import jax.numpy as jnp
from jax import lax
from jax.experimental import pallas as pl
from jax.experimental.pallas import tpu as pltpu
from jax.sharding import PartitionSpec as P

BF16 = jnp.bfloat16
F32 = jnp.float32
SUB = 8
LANES = 128
BOTH = ("seq", "chan")


def spread_rows(row):
    return jnp.broadcast_to(row, (SUB, row.shape[-1]))


def runs(ref, chunk):
    length = ref.shape[1] // SUB
    return [ref[chunk, pl.ds(i, SUB, stride=length), :] for i in range(length)]


def powers(rate, length):
    once = jnp.exp(rate * length)
    twice = once * once
    return once, twice, twice * twice


def raised(steps, pows, m):
    result = jnp.where(steps % 2 == 1, spread_rows(pows[0][m : m + 1]), 1.0)
    result = result * jnp.where(steps // 2 % 2 == 1, spread_rows(pows[1][m : m + 1]), 1.0)
    return result * jnp.where(steps >= 4, spread_rows(pows[2][m : m + 1]), 1.0)


def state_kernel(total, pieces, *refs):
    hbm, (state_ref, *near, k_ref, v_ref, sems) = refs[:6], refs[6:]
    x_ref, rate_ref, gain_ref, q_ref, skip_ref = near
    modes, width = rate_ref.shape
    length = x_ref.shape[1] // SUB
    part = width // pieces

    def copies(piece):
        lanes = pl.ds(piece * part, part)
        pairs = zip(hbm[:4], (k_ref, v_ref, rate_ref, gain_ref))
        return [
            pltpu.make_async_copy(src.at[:, lanes], dst.at[:, lanes], sems.at[piece, j])
            for j, (src, dst) in enumerate(pairs)
        ]

    whole = [pltpu.make_async_copy(src, dst, sems.at[pieces, j]) for j, (src, dst) in enumerate(zip(hbm[4:6], (q_ref, skip_ref)))]
    for piece in range(pieces):
        for copy in copies(piece):
            copy.start()
    for copy in whole:
        copy.start()
    left = SUB - 1 - lax.broadcasted_iota(jnp.int32, (SUB, LANES), 0)
    for piece in range(pieces):
        for copy in copies(piece):
            copy.wait()

        @pl.loop(0, part // LANES)
        def _(chunk):
            chunk = piece * (part // LANES) + chunk
            lanes = pl.ds(pl.multiple_of(chunk * LANES, LANES), LANES)
            x_ref[chunk] = k_ref[:, lanes].astype(F32) * v_ref[:, lanes].astype(F32)
            gain_ref[:, lanes] = gain_ref[:, lanes] * jnp.sqrt(rate_ref[:, lanes] * (2.0 / total))
            x = runs(x_ref, chunk)
            rate = rate_ref[:, lanes] * (-1.0 / total)
            decay = jnp.exp(rate)
            pows = powers(rate, length)
            rows = []
            for m in range(modes):
                d = spread_rows(decay[m : m + 1])
                state = x[0]
                for i in range(1, length):
                    state = state * d + x[i]
                rows.append(jnp.sum(state * raised(left, pows, m), axis=0, keepdims=True))
            state_ref[:, lanes] = jnp.concatenate(rows, axis=0).astype(BF16)

    for copy in whole:
        copy.wait()


def local_kernel(total, window, x_ref, rate_ref, gain_ref, skip_ref, *rest):
    base_ref = rest[-1]
    modes, width = rate_ref.shape
    length = x_ref.shape[1] // SUB
    block = lax.broadcasted_iota(jnp.int32, (SUB, LANES), 0)

    @pl.loop(window[0], window[1])
    def _(chunk):
        lanes = pl.ds(pl.multiple_of(chunk * LANES, LANES), LANES)
        x = runs(x_ref, chunk)
        rate = rate_ref[:, lanes] * (-1.0 / total)
        gain = gain_ref[:, lanes]
        decay = jnp.exp(rate)
        pows = powers(rate, length)
        y = [spread_rows(skip_ref[:, lanes]) * x[i] for i in range(length)]
        power = gain
        for j in range(length):
            tap = spread_rows(jnp.sum(power, axis=0, keepdims=True))
            for i in range(j, length):
                y[i] = y[i] + tap * x[i - j]
            power = power * decay
        for m in range(modes):
            d = spread_rows(decay[m : m + 1])
            state = x[0]
            for i in range(1, length):
                state = state * d + x[i]
            state = jnp.where(block >= 1, pltpu.roll(state, 1, 0), 0.0)
            for shift, step in zip((1, 2, 4), pows):
                moved_on = jnp.where(block >= shift, pltpu.roll(state, shift, 0), 0.0)
                state = state + spread_rows(step[m : m + 1]) * moved_on
            state = state * spread_rows(gain[m : m + 1])
            for i in range(length):
                state = state * d
                y[i] = y[i] + state
        for i in range(length):
            base_ref[chunk, pl.ds(i, SUB, stride=length), :] = y[i]


def carry_kernel(total, odd_ref, q_ref, base_ref, below_ref, further_ref, first_ref, rate_ref, gain_ref, out_ref, y_ref):
    modes, width = rate_ref.shape
    length = y_ref.shape[0] // SUB
    rows = y_ref.shape[0]
    block = lax.broadcasted_iota(jnp.int32, (SUB, LANES), 0)

    @pl.loop(0, width // LANES)
    def _(chunk):
        lanes = pl.ds(pl.multiple_of(chunk * LANES, LANES), LANES)
        rate = rate_ref[:, lanes] * (-1.0 / total)
        pows = powers(rate, length)
        start = below_ref[:, lanes].astype(F32) + further_ref[:, lanes].astype(F32) * jnp.exp(rate * (2 * rows))
        later = start * jnp.exp(rate * rows) + first_ref[:, lanes].astype(F32)
        start = jnp.where(odd_ref[0] == 1, later, start) * gain_ref[:, lanes]
        decay = jnp.exp(rate)
        y = runs(base_ref, chunk)
        for m in range(modes):
            d = spread_rows(decay[m : m + 1])
            state = spread_rows(start[m : m + 1]) * raised(block, pows, m)
            for i in range(length):
                state = state * d
                y[i] = y[i] + state
        for i in range(length):
            y_ref[pl.ds(i, SUB, stride=length), :] = y[i]
        out_ref[:, lanes] = (y_ref[...] * q_ref[:, lanes].astype(F32)).astype(BF16)


def run(kernel, outs, ops, mib, args, scratch=(), scalars=(), near=True, aliases={}):
    space = pltpu.VMEM if near else pl.ANY
    return pl.pallas_call(
        kernel,
        out_shape=[jax.ShapeDtypeStruct(shape, kind) for shape, kind in outs],
        in_specs=[pl.BlockSpec(memory_space=pltpu.SMEM)] * len(scalars)
        + [pl.BlockSpec(memory_space=space)] * len(args),
        out_specs=[pl.BlockSpec(memory_space=pltpu.VMEM)] * len(outs),
        scratch_shapes=scratch,
        input_output_aliases=aliases,
        compiler_params=pltpu.CompilerParams(vmem_limit_bytes=mib * 1024 * 1024),
        cost_estimate=pl.CostEstimate(
            flops=int(ops * args[0].size), bytes_accessed=4 * args[0].size, transcendentals=0
        ),
    )(*scalars, *args)


def matmul(x, w):
    return jnp.dot(x, w, preferred_element_type=F32)


def moved(x, axes, pairs, name):
    with jax.named_scope(name):
        return lax.ppermute(x, axes, pairs)


def fence(*xs):
    return lax.optimization_barrier(xs)


def general(base_of, hidden_of, state, w_out, fade, rows, index, parts):
    states = lax.all_gather(state, "seq", axis=0)
    entering = jnp.zeros(state.shape, F32)
    for b in range(parts):
        entering = jnp.where(b < index, entering * fade(rows) + states[b].astype(F32), entering)
    nothing = jnp.zeros_like(state)
    hidden = hidden_of(base_of((0, 16)), entering, nothing, nothing, jnp.int32(0))
    spread = matmul(lax.all_gather(hidden, "seq", axis=0, tiled=True), w_out)
    partial_value = lax.all_to_all(spread, "seq", split_axis=0, concat_axis=1, tiled=True)
    summed = lax.psum_scatter(partial_value, "chan", scatter_dimension=1, tiled=True)
    return summed.astype(BF16)


def lined(base_of, hidden_of, state, w_out, fade, rows, index):
    depth = 4
    z, y = index // 2, index % 2

    def along(x, moves, name):
        return moved(x, "seq", [(a * 2 + b, c * 2 + b) for a, c in moves for b in range(2)], name)

    def across(x, planes, name):
        return moved(x, "seq", [(a * 2 + b, a * 2 + 1 - b) for a in planes for b in range(2)], name)

    def shift(by):
        return [(a, a + by) for a in range(depth) if 0 <= a + by < depth]

    every = range(depth)
    other = across(state, every, "state_y")
    other, *base = fence(other, *base_of((0, 2)))
    first = jnp.where(y == 0, state, other)
    second = jnp.where(y == 0, other, state)
    plane = first.astype(F32) * fade(rows) + second.astype(F32)
    below = along(plane.astype(BF16), shift(1), "state_1")
    below, *base = fence(below, *base_of((2, 9), base))
    two_below = (plane + below.astype(F32) * fade(2 * rows)).astype(BF16)
    further = along(two_below, shift(2), "state_2")
    base = base_of((9, 16), base)
    hidden = hidden_of(base, below, further, first, y)

    chan = lax.axis_index("chan")
    side, core = chan // 2, chan % 2
    pairwise = [(0, 1), (1, 0), (2, 3), (3, 2)]
    inner, outward = [(1, 2), (2, 1)], [(1, 0), (2, 3)]
    near_y = across(hidden, every, "near_y")
    one = along(hidden, pairwise, "one")
    middle = along(hidden, inner, "middle")
    one, middle, near_y = fence(one, middle, near_y)

    one_y = across(one, every, "one_y")
    given = along(one, inner, "given")
    out2 = along(middle, outward, "out2")
    given, out2, one_y, late_y = fence(given, out2, one_y, near_y[:, hidden.shape[1] // 2 :])

    at_end = z % 3 == 0
    two = jnp.where(at_end, out2, given)
    two_y = across(two, every, "two_y")
    out3 = along(given, outward, "out3")
    split = hidden.shape[1] // 2
    middle_y = along(late_y, inner, "middle_y")

    flip = [(c, c ^ 1) for c in range(4)]
    turn = [(c, c ^ 2) for c in range(4)]

    def owned(dy):
        pairs = []
        for a, b, x in itertools.product(every, range(2), range(2)):
            for k in range(2):
                apart = 2 + (x ^ (a // 2)) if k == dy else x
                pairs.append(((a * 2 + b) * 4 + x * 2 + k, ((a ^ apart) * 2 + (b ^ dy)) * 4 + a))
        return pairs

    def turned(here, first, second, pairs, name):
        keep = jnp.where(here, first, second)
        return keep, moved(jnp.where(here, second, first).astype(BF16), "chan", pairs, name)

    def far(first, second, dy):
        parts = jnp.stack([first.astype(BF16), second.astype(BF16)])
        given = moved(parts, "chan", [(1 - dy, dy), (3 - dy, 2 + dy)], f"core_far{dy}")
        parts = (parts.astype(F32) + given.astype(F32)).astype(BF16)
        return turned(side == z // 2, parts[0], parts[1], [(dy, 2 + dy), (2 + dy, dy)], f"side_far{dy}")

    ready = [[matmul(x, w_out) for x in (hidden, near_y)], [matmul(x, w_out) for x in (one, one_y)]]
    keep = jnp.stack([jnp.where(core == 0, second, first) for first, second in ready])
    send = jnp.stack([jnp.where(core == 0, first, second).astype(BF16) for first, second in ready])
    close = keep + moved(send, "chan", flip, "core_close").astype(F32)
    close_keep, close_side = turned(side == 0, close[0], close[1], turn, "side_close")

    out3, two_y, middle_y = fence(out3, two_y, middle_y)
    three = jnp.where(at_end, out3, middle)
    three_y = across(three[:, :split], every, "three_y")
    out_y = along(two_y[:, split:], outward, "out_y")
    with_three = matmul(three, w_out)
    far_keep, far_side = far(matmul(two, w_out), with_three, 0)
    close_tile = (close_keep + close_side.astype(F32)).astype(BF16)
    tile = (far_keep.astype(F32) + far_side.astype(F32)).astype(BF16)
    mixed = jnp.where(core == 0, tile, close_tile)
    three_y, out_y, mixed, close_tile = fence(three_y, out_y, mixed, close_tile)
    same = moved(mixed, BOTH, owned(0), "own_0")
    with_three_y = matmul(three_y, w_out[:split]) + matmul(jnp.where(at_end, out_y, middle_y), w_out[split:])
    far_keep, far_side = far(matmul(two_y, w_out), with_three_y, 1)
    tile = (far_keep.astype(F32) + far_side.astype(F32)).astype(BF16)
    cross = moved(jnp.where(core == 1, tile, close_tile), BOTH, owned(1), "own_1")
    low = jnp.where(y == 0, same, cross)
    high = jnp.where(y == 0, cross, same)
    return jnp.concatenate([low, high], axis=1)


def local(q_proj, k_proj, v_proj, residues, rates, skip_gain, w_out):
    rows, width = q_proj.shape
    parts = lax.axis_size("seq")
    index = lax.axis_index("seq")
    total = rows * parts
    modes = rates.shape[1]
    res_t, rate_t = residues.T, rates.T
    pieces = 4
    tall, thin = (rows, width), (modes, width)
    chunks = (width // LANES, rows, LANES)
    state, x, rate_near, gain, q_near, skip = run(
        functools.partial(state_kernel, total, pieces),
        [(thin, BF16), (chunks, F32), (thin, F32), (thin, F32), (tall, BF16), ((1, width), F32)],
        48,
        60,
        [k_proj, v_proj, rate_t, res_t, q_proj, skip_gain[None, :]],
        [pltpu.VMEM(tall, BF16), pltpu.VMEM(tall, BF16), pltpu.SemaphoreType.DMA((pieces + 1, 4))],
        near=False,
    )

    def base_of(window, filled=()):
        count = width // LANES
        window = (window[0] * count // 16, window[1] * count // 16)
        return run(
            functools.partial(local_kernel, total, window),
            [(chunks, F32)],
            100 * (window[1] - window[0]) / count,
            16,
            [x, rate_near, gain, skip, *filled],
            aliases={4: 0} if filled else {},
        )

    def hidden_of(base, below, further, first, odd):
        return run(
            functools.partial(carry_kernel, total),
            [(tall, BF16)],
            32,
            16,
            [q_near, *base, below, further, first, rate_near, gain],
            [pltpu.VMEM((rows, LANES), F32)],
            scalars=(odd.astype(jnp.int32)[None],),
        )[0]

    def fade(steps):
        return jnp.exp(rate_t * (-float(steps) / total))

    if parts == 8 and lax.axis_size("chan") == 4:
        return lined(base_of, hidden_of, state, w_out, fade, rows, index)
    return general(base_of, hidden_of, state, w_out, fade, rows, index, parts)


def solution(mesh):
    return jax.shard_map(
        local,
        mesh=mesh,
        in_specs=(
            P("seq", "chan"),
            P("seq", "chan"),
            P("seq", "chan"),
            P("chan", None),
            P("chan", None),
            P("chan"),
            P("chan", "seq"),
        ),
        out_specs=P("seq", "chan"),
        check_vma=False,
    )
```

```python
import functools
import itertools

import jax
import jax.numpy as jnp
from jax import lax
from jax.experimental import pallas as pl
from jax.experimental.pallas import tpu as pltpu
from jax.sharding import PartitionSpec as P

BF16 = jnp.bfloat16
F32 = jnp.float32
SUB = 8
LANES = 128
BOTH = ("seq", "chan")


def spread_rows(row):
    return jnp.broadcast_to(row, (SUB, row.shape[-1]))


def runs(ref, chunk):
    length = ref.shape[1] // SUB
    return [ref[chunk, pl.ds(i, SUB, stride=length), :] for i in range(length)]


def powers(rate, length):
    once = jnp.exp(rate * length)
    twice = once * once
    return once, twice, twice * twice


def raised(steps, pows, m):
    result = jnp.where(steps % 2 == 1, spread_rows(pows[0][m : m + 1]), 1.0)
    result = result * jnp.where(steps // 2 % 2 == 1, spread_rows(pows[1][m : m + 1]), 1.0)
    return result * jnp.where(steps >= 4, spread_rows(pows[2][m : m + 1]), 1.0)


def state_kernel(total, pieces, *refs):
    hbm, (state_ref, *near, k_ref, v_ref, sems) = refs[:5], refs[5:]
    x_ref, rate_ref, gain_ref, skip_ref = near
    modes, width = rate_ref.shape
    length = x_ref.shape[1] // SUB
    part = width // pieces

    def copies(piece):
        lanes = pl.ds(piece * part, part)
        pairs = zip(hbm[:4], (k_ref, v_ref, rate_ref, gain_ref))
        return [
            pltpu.make_async_copy(src.at[:, lanes], dst.at[:, lanes], sems.at[piece, j])
            for j, (src, dst) in enumerate(pairs)
        ]

    whole = [pltpu.make_async_copy(hbm[4], skip_ref, sems.at[pieces, 0])]
    for piece in range(pieces):
        for copy in copies(piece):
            copy.start()
    for copy in whole:
        copy.start()
    left = SUB - 1 - lax.broadcasted_iota(jnp.int32, (SUB, LANES), 0)
    for piece in range(pieces):
        for copy in copies(piece):
            copy.wait()

        @pl.loop(0, part // LANES)
        def _(chunk):
            chunk = piece * (part // LANES) + chunk
            lanes = pl.ds(pl.multiple_of(chunk * LANES, LANES), LANES)
            x_ref[chunk] = k_ref[:, lanes].astype(F32) * v_ref[:, lanes].astype(F32)
            gain_ref[:, lanes] = gain_ref[:, lanes] * jnp.sqrt(rate_ref[:, lanes] * (2.0 / total))
            x = runs(x_ref, chunk)
            rate = rate_ref[:, lanes] * (-1.0 / total)
            decay = jnp.exp(rate)
            pows = powers(rate, length)
            rows = []
            for m in range(modes):
                d = spread_rows(decay[m : m + 1])
                state = x[0]
                for i in range(1, length):
                    state = state * d + x[i]
                rows.append(jnp.sum(state * raised(left, pows, m), axis=0, keepdims=True))
            state_ref[:, lanes] = jnp.concatenate(rows, axis=0).astype(BF16)

    for copy in whole:
        copy.wait()


def local_kernel(total, window, x_ref, rate_ref, gain_ref, skip_ref, *rest):
    base_ref = rest[-1]
    modes, width = rate_ref.shape
    length = x_ref.shape[1] // SUB
    block = lax.broadcasted_iota(jnp.int32, (SUB, LANES), 0)

    @pl.loop(window[0], window[1])
    def _(chunk):
        lanes = pl.ds(pl.multiple_of(chunk * LANES, LANES), LANES)
        x = runs(x_ref, chunk)
        rate = rate_ref[:, lanes] * (-1.0 / total)
        gain = gain_ref[:, lanes]
        decay = jnp.exp(rate)
        pows = powers(rate, length)
        y = [spread_rows(skip_ref[:, lanes]) * x[i] for i in range(length)]
        power = gain
        for j in range(length):
            tap = spread_rows(jnp.sum(power, axis=0, keepdims=True))
            for i in range(j, length):
                y[i] = y[i] + tap * x[i - j]
            power = power * decay
        for m in range(modes):
            d = spread_rows(decay[m : m + 1])
            state = x[0]
            for i in range(1, length):
                state = state * d + x[i]
            state = jnp.where(block >= 1, pltpu.roll(state, 1, 0), 0.0)
            for shift, step in zip((1, 2, 4), pows):
                moved_on = jnp.where(block >= shift, pltpu.roll(state, shift, 0), 0.0)
                state = state + spread_rows(step[m : m + 1]) * moved_on
            state = state * spread_rows(gain[m : m + 1])
            for i in range(length):
                state = state * d
                y[i] = y[i] + state
        for i in range(length):
            base_ref[chunk, pl.ds(i, SUB, stride=length), :] = y[i]


def carry_kernel(total, odd_ref, q_ref, base_ref, below_ref, further_ref, first_ref, rate_ref, gain_ref, out_ref, y_ref):
    modes, width = rate_ref.shape
    length = y_ref.shape[0] // SUB
    rows = y_ref.shape[0]
    block = lax.broadcasted_iota(jnp.int32, (SUB, LANES), 0)

    @pl.loop(0, width // LANES)
    def _(chunk):
        lanes = pl.ds(pl.multiple_of(chunk * LANES, LANES), LANES)
        rate = rate_ref[:, lanes] * (-1.0 / total)
        pows = powers(rate, length)
        start = below_ref[:, lanes].astype(F32) + further_ref[:, lanes].astype(F32) * jnp.exp(rate * (2 * rows))
        later = start * jnp.exp(rate * rows) + first_ref[:, lanes].astype(F32)
        start = jnp.where(odd_ref[0] == 1, later, start) * gain_ref[:, lanes]
        decay = jnp.exp(rate)
        y = runs(base_ref, chunk)
        for m in range(modes):
            d = spread_rows(decay[m : m + 1])
            state = spread_rows(start[m : m + 1]) * raised(block, pows, m)
            for i in range(length):
                state = state * d
                y[i] = y[i] + state
        for i in range(length):
            y_ref[pl.ds(i, SUB, stride=length), :] = y[i]
        out_ref[:, lanes] = (y_ref[...] * q_ref[:, lanes].astype(F32)).astype(BF16)


def run(kernel, outs, ops, mib, args, scratch=(), scalars=(), near=True, aliases={}):
    space = pltpu.VMEM if near else pl.ANY
    return pl.pallas_call(
        kernel,
        out_shape=[jax.ShapeDtypeStruct(shape, kind) for shape, kind in outs],
        in_specs=[pl.BlockSpec(memory_space=pltpu.SMEM)] * len(scalars)
        + [pl.BlockSpec(memory_space=space)] * len(args),
        out_specs=[pl.BlockSpec(memory_space=pltpu.VMEM)] * len(outs),
        scratch_shapes=scratch,
        input_output_aliases=aliases,
        compiler_params=pltpu.CompilerParams(vmem_limit_bytes=mib * 1024 * 1024),
        cost_estimate=pl.CostEstimate(
            flops=int(ops * args[0].size), bytes_accessed=4 * args[0].size, transcendentals=0
        ),
    )(*scalars, *args)


def matmul(x, w):
    return jnp.dot(x, w, preferred_element_type=F32)


def moved(x, axes, pairs, name):
    with jax.named_scope(name):
        return lax.ppermute(x, axes, pairs)


def fence(*xs):
    return lax.optimization_barrier(xs)


def general(base_of, hidden_of, state, w_out, fade, rows, index, parts):
    states = lax.all_gather(state, "seq", axis=0)
    entering = jnp.zeros(state.shape, F32)
    for b in range(parts):
        entering = jnp.where(b < index, entering * fade(rows) + states[b].astype(F32), entering)
    nothing = jnp.zeros_like(state)
    hidden = hidden_of(base_of((0, 16)), entering, nothing, nothing, jnp.int32(0))
    spread = matmul(lax.all_gather(hidden, "seq", axis=0, tiled=True), w_out)
    partial_value = lax.all_to_all(spread, "seq", split_axis=0, concat_axis=1, tiled=True)
    summed = lax.psum_scatter(partial_value, "chan", scatter_dimension=1, tiled=True)
    return summed.astype(BF16)


def lined(base_of, hidden_of, state, w_out, fade, rows, index):
    depth = 4
    z, y = index // 2, index % 2

    def along(x, moves, name):
        return moved(x, "seq", [(a * 2 + b, c * 2 + b) for a, c in moves for b in range(2)], name)

    def across(x, planes, name):
        return moved(x, "seq", [(a * 2 + b, a * 2 + 1 - b) for a in planes for b in range(2)], name)

    def shift(by):
        return [(a, a + by) for a in range(depth) if 0 <= a + by < depth]

    every = range(depth)
    other = across(state, every, "state_y")
    other, *base = fence(other, *base_of((0, 2)))
    first = jnp.where(y == 0, state, other)
    second = jnp.where(y == 0, other, state)
    plane = first.astype(F32) * fade(rows) + second.astype(F32)
    below = along(plane.astype(BF16), shift(1), "state_1")
    below, *base = fence(below, *base_of((2, 9), base))
    two_below = (plane + below.astype(F32) * fade(2 * rows)).astype(BF16)
    further = along(two_below, shift(2), "state_2")
    base = base_of((9, 16), base)
    hidden = hidden_of(base, below, further, first, y)

    chan = lax.axis_index("chan")
    side, core = chan // 2, chan % 2
    pairwise = [(0, 1), (1, 0), (2, 3), (3, 2)]
    inner, outward = [(1, 2), (2, 1)], [(1, 0), (2, 3)]
    near_y = across(hidden, every, "near_y")
    one = along(hidden, pairwise, "one")
    middle = along(hidden, inner, "middle")
    one, middle, near_y = fence(one, middle, near_y)

    one_y = across(one, every, "one_y")
    given = along(one, inner, "given")
    out2 = along(middle, outward, "out2")
    given, out2, one_y, late_y = fence(given, out2, one_y, near_y[:, hidden.shape[1] // 2 :])

    at_end = z % 3 == 0
    two = jnp.where(at_end, out2, given)
    two_y = across(two, every, "two_y")
    out3 = along(given, outward, "out3")
    split = hidden.shape[1] // 2
    middle_y = along(late_y, inner, "middle_y")

    flip = [(c, c ^ 1) for c in range(4)]
    turn = [(c, c ^ 2) for c in range(4)]

    def owned(dy):
        pairs = []
        for a, b, x in itertools.product(every, range(2), range(2)):
            for k in range(2):
                apart = 2 + (x ^ (a // 2)) if k == dy else x
                pairs.append(((a * 2 + b) * 4 + x * 2 + k, ((a ^ apart) * 2 + (b ^ dy)) * 4 + a))
        return pairs

    def turned(here, first, second, pairs, name):
        keep = jnp.where(here, first, second)
        return keep, moved(jnp.where(here, second, first).astype(BF16), "chan", pairs, name)

    def far(first, second, dy):
        parts = jnp.stack([first.astype(BF16), second.astype(BF16)])
        given = moved(parts, "chan", [(1 - dy, dy), (3 - dy, 2 + dy)], f"core_far{dy}")
        parts = (parts.astype(F32) + given.astype(F32)).astype(BF16)
        return turned(side == z // 2, parts[0], parts[1], [(dy, 2 + dy), (2 + dy, dy)], f"side_far{dy}")

    ready = [[matmul(x, w_out) for x in (hidden, near_y)], [matmul(x, w_out) for x in (one, one_y)]]
    keep = jnp.stack([jnp.where(core == 0, second, first) for first, second in ready])
    send = jnp.stack([jnp.where(core == 0, first, second).astype(BF16) for first, second in ready])
    close = keep + moved(send, "chan", flip, "core_close").astype(F32)
    close_keep, close_side = turned(side == 0, close[0], close[1], turn, "side_close")

    out3, two_y, middle_y = fence(out3, two_y, middle_y)
    three = jnp.where(at_end, out3, middle)
    three_y = across(three[:, :split], every, "three_y")
    out_y = along(two_y[:, split:], outward, "out_y")
    with_three = matmul(three, w_out)
    far_keep, far_side = far(matmul(two, w_out), with_three, 0)
    close_tile = (close_keep + close_side.astype(F32)).astype(BF16)
    tile = (far_keep.astype(F32) + far_side.astype(F32)).astype(BF16)
    mixed = jnp.where(core == 0, tile, close_tile)
    three_y, out_y, mixed, close_tile = fence(three_y, out_y, mixed, close_tile)
    same = moved(mixed, BOTH, owned(0), "own_0")
    with_three_y = matmul(three_y, w_out[:split]) + matmul(jnp.where(at_end, out_y, middle_y), w_out[split:])
    far_keep, far_side = far(matmul(two_y, w_out), with_three_y, 1)
    tile = (far_keep.astype(F32) + far_side.astype(F32)).astype(BF16)
    cross = moved(jnp.where(core == 1, tile, close_tile), BOTH, owned(1), "own_1")
    low = jnp.where(y == 0, same, cross)
    high = jnp.where(y == 0, cross, same)
    return jnp.concatenate([low, high], axis=1)


def local(q_proj, k_proj, v_proj, residues, rates, skip_gain, w_out):
    rows, width = q_proj.shape
    parts = lax.axis_size("seq")
    index = lax.axis_index("seq")
    total = rows * parts
    modes = rates.shape[1]
    res_t, rate_t = residues.T, rates.T
    pieces = 4
    tall, thin = (rows, width), (modes, width)
    chunks = (width // LANES, rows, LANES)
    state, x, rate_near, gain, skip = run(
        functools.partial(state_kernel, total, pieces),
        [(thin, BF16), (chunks, F32), (thin, F32), (thin, F32), ((1, width), F32)],
        48,
        60,
        [k_proj, v_proj, rate_t, res_t, skip_gain[None, :]],
        [pltpu.VMEM(tall, BF16), pltpu.VMEM(tall, BF16), pltpu.SemaphoreType.DMA((pieces + 1, 4))],
        near=False,
    )

    def base_of(window, filled=()):
        count = width // LANES
        window = (window[0] * count // 16, window[1] * count // 16)
        return run(
            functools.partial(local_kernel, total, window),
            [(chunks, F32)],
            100 * (window[1] - window[0]) / count,
            16,
            [x, rate_near, gain, skip, *filled],
            aliases={4: 0} if filled else {},
        )

    def hidden_of(base, below, further, first, odd):
        return run(
            functools.partial(carry_kernel, total),
            [(tall, BF16)],
            32,
            16,
            [q_proj, *base, below, further, first, rate_near, gain],
            [pltpu.VMEM((rows, LANES), F32)],
            scalars=(odd.astype(jnp.int32)[None],),
        )[0]

    def fade(steps):
        return jnp.exp(rate_t * (-float(steps) / total))

    if parts == 8 and lax.axis_size("chan") == 4:
        return lined(base_of, hidden_of, state, w_out, fade, rows, index)
    return general(base_of, hidden_of, state, w_out, fade, rows, index, parts)


def solution(mesh):
    return jax.shard_map(
        local,
        mesh=mesh,
        in_specs=(
            P("seq", "chan"),
            P("seq", "chan"),
            P("seq", "chan"),
            P("chan", None),
            P("chan", None),
            P("chan"),
            P("chan", "seq"),
        ),
        out_specs=P("seq", "chan"),
        check_vma=False,
    )
```
